256 devices in a mesh: ctx: 64 (over y, z, core), batch: 4 (over x).
Axes of the slice: x: 4, y: 4, z: 8, core: 2. Of those that a mesh axis runs over, the one named last changes fastest.
Arguments:
- cache_keys: bfloat16 [131072, 4096], P('ctx', 'batch'), parts along dimension 1
- cache_values: bfloat16 [131072, 4096], P('ctx', 'batch'), parts along dimension 1, may hold values from -6 to 6
- sketch_matrix: bfloat16 [1024, 160], replicated, may hold values from -0.1875 to 0.1875
- queries: bfloat16 [2, 64, 4096], P(None, 'batch'), parts along dimension 1
- visible: int32 [2, 64], P(None, 'batch'), parts along dimension 1, may hold values from 65536 to 131072, as said below
Outputs:
- rank_keys: bfloat16 [131072, 640], P('ctx', 'batch'), parts along dimension 1
- attended: bfloat16 [2, 64, 4096], P(None, 'batch'), parts along dimension 1
The draws below stay inside these ranges and needn't reach their ends.
There are 4 independent parts, one for each index of `batch`. The reference program is written for one: setup_inputs(seed, part) draws one part's arguments, and reference() takes and returns one part's arrays. A program takes and returns all parts, laid end to end along the dimension named above; an argument that names none is the same for every part. Nothing has to cross between parts.
Inputs may be any that keep to these rules, and one draw needn't show every extreme that they name: `visible`: row 0 sees all 131072 positions in every step.
All inputs are finite; a program needn't handle non-finite values.
Results may differ from the reference program's by a relative error of at most 0.03.
The reference program's roundings to bfloat16 on the way (of `sketch_rows`, `basis`, `projected` and `weights`) count: a program that leaves them out, or rounds other values in their place, can miss the bound.
Values may be sent and summed in bfloat16 or wider, within the bound.
No kernel may reach another device: no remote copies, remote signals or barrier semaphores. Data moves between devices by JAX's collectives and lax.ppermute only.
A program may use at most 128 MiB of HBM per device.

```python
import math
import jax
import jax.numpy as jnp
from jax import lax

HEADS = 32
KV_HEADS = 8
HEAD_DIM = 128
RANK = 160
ROWS = 16
STEPS = 2
KEY_WIDTH = 1024
CONTEXT = 131072


def anchor_rows(key):
    first = jax.random.normal(jax.random.fold_in(key, 101), (8, KEY_WIDTH), jnp.float32)
    other = jax.random.normal(jax.random.fold_in(key, 102), (8, KEY_WIDTH), jnp.float32)
    second = jnp.sqrt(1.0) * other
    return jnp.stack([first, second], axis=1).reshape(16, KEY_WIDTH)


def draw_cache_keys(key, part):
    anchors = anchor_rows(key)
    key = jax.random.fold_in(key, 3)
    drawn = jax.random.normal(jax.random.fold_in(key, 1), (CONTEXT, KEY_WIDTH), jnp.float32)
    whole = jnp.concatenate([anchors, drawn[16:]], axis=0)
    return jnp.clip(whole, -8.0, 8.0).astype(jnp.bfloat16)


def draw_queries(key, part):
    key = jax.random.fold_in(key, 5)
    base = 8.0 * jax.random.normal(key, (STEPS, ROWS, HEADS * HEAD_DIM), jnp.float32)
    base = jnp.clip(base, -48.0, 48.0)
    return base.astype(jnp.bfloat16)


def draw_visible(key, part):
    key = jax.random.fold_in(key, 7)
    half = CONTEXT // 2
    counts = half + jax.random.randint(key, (STEPS, ROWS), 0, CONTEXT - half + 1, jnp.int32)
    counts = counts.at[:, 0].set(CONTEXT)
    return counts.astype(jnp.int32)


def steps_of(rng, shape, shards, smallest, largest):
    loudness = 1.0
    for dim, shards_of in shards:
        draws = jax.random.uniform(jax.random.fold_in(jax.random.fold_in(rng, 6), dim), (shards_of,), jnp.float32, smallest / len(shards), largest / len(shards))
        loudness = loudness * jnp.repeat(jnp.exp(draws), shape[dim] // shards_of).reshape((-1,) + (1,) * (len(shape) - 1 - dim))
    return loudness


def bell_draw(own_key, shape, spread, most, cuts=(), kind=jnp.bfloat16):
    factor_of = steps_of(own_key, shape, cuts, -0.22, 0.18) if cuts else 1.0
    values = jax.random.normal(own_key, shape, jnp.float32) * spread * factor_of
    return jnp.minimum(jnp.maximum(values, -most), most).astype(kind)


def setup_inputs(seed: int = 0, part: int = 0) -> dict:
    streams_of = jax.random.split(jax.random.key(seed), 6)
    part_splits = jax.random.split(jax.random.fold_in(streams_of[5], part), 6)
    return {
        "cache_keys": draw_cache_keys(jax.random.fold_in(jax.random.fold_in(streams_of[5], part), 71), part),
        "cache_values": bell_draw(part_splits[1], (CONTEXT, KEY_WIDTH), 1.0, 6.0, ((0, 64),)),
        "sketch_matrix": bell_draw(streams_of[2], (KEY_WIDTH, RANK), KEY_WIDTH ** -0.5, 0.1875),
        "queries": draw_queries(jax.random.fold_in(jax.random.fold_in(streams_of[5], part), 71), part),
        "visible": draw_visible(jax.random.fold_in(jax.random.fold_in(streams_of[5], part), 71), part),
    }


def reference(cache_keys, cache_values, sketch_matrix, queries, visible):
    sketch_rows = jnp.dot(cache_keys.astype(jnp.float32), sketch_matrix.astype(jnp.float32), preferred_element_type=jnp.float32).astype(jnp.bfloat16)
    power = jnp.dot(cache_keys.T.astype(jnp.float32), sketch_rows.astype(jnp.float32), preferred_element_type=jnp.float32)
    gram = jnp.dot(power.T.astype(jnp.float32), power.astype(jnp.float32), precision=lax.Precision.HIGHEST, preferred_element_type=jnp.float32)
    lower = jnp.linalg.cholesky(gram)
    basis = lax.linalg.triangular_solve(lower, power, left_side=False, lower=True, transpose_a=True).astype(jnp.bfloat16)
    rank_keys = jnp.dot(cache_keys.astype(jnp.float32), basis.astype(jnp.float32), preferred_element_type=jnp.float32).astype(jnp.bfloat16)
    group_size = HEADS // KV_HEADS
    basis_groups = basis.reshape(KV_HEADS, HEAD_DIM, RANK).astype(jnp.float32)
    query_groups = queries.reshape(STEPS, ROWS, KV_HEADS, group_size, HEAD_DIM).astype(jnp.float32)
    projected = jnp.einsum('trgqd,gdk->trgqk', query_groups, basis_groups).astype(jnp.bfloat16)
    projected = projected.reshape(STEPS * ROWS, HEADS, RANK)
    value_groups = cache_values.reshape(CONTEXT, KV_HEADS, HEAD_DIM).transpose(1, 0, 2)
    keys_major = rank_keys.T
    positions = jnp.arange(CONTEXT, dtype=jnp.int32)
    limits = visible.reshape(STEPS * ROWS).astype(jnp.int32)
    score_scale = 1.0 / math.sqrt(HEAD_DIM)

    def one_row(operands):
        query_rank, limit = operands
        scores = jnp.dot(query_rank.astype(jnp.float32), keys_major.astype(jnp.float32), preferred_element_type=jnp.float32) * score_scale
        masked = positions < limit
        scores = jnp.where(masked[None, :], scores, jnp.float32(-1e+30))
        top = lax.optimization_barrier(jnp.max(scores, axis=1, keepdims=True))
        expo = jnp.where(masked[None, :], jnp.exp(scores - top), jnp.float32(0.0))
        total = lax.optimization_barrier(jnp.sum(expo, axis=1))
        weights = expo.astype(jnp.bfloat16).reshape(KV_HEADS, group_size, CONTEXT)
        outputs = jnp.stack([jnp.dot(weights[group].astype(jnp.float32), value_groups[group].astype(jnp.float32), preferred_element_type=jnp.float32) for group in range(KV_HEADS)])
        outputs = outputs.reshape(HEADS, HEAD_DIM) / total[:, None]
        return outputs.astype(jnp.bfloat16)
    attended = lax.map(one_row, (projected, limits)).reshape(STEPS, ROWS, HEADS * HEAD_DIM)
    return (rank_keys, attended)
```

```python
import math

import jax
import jax.numpy as jnp
from jax import lax
from jax.experimental import pallas as pl
from jax.experimental.pallas import tpu as pltpu
from jax.sharding import PartitionSpec as P

HEADS = 32
KV_HEADS = 8
HEAD_DIM = 128
RANK = 160
ROWS = 16
STEPS = 2
WIDTH = KV_HEADS * HEAD_DIM
GROUP = HEADS // KV_HEADS
QUERIES = STEPS * ROWS
STACKED = GROUP * QUERIES
NY = 4
NZ = 8
NC = 2
HALF = KV_HEADS // NC
CHUNK = HALF * STACKED // (NY * NZ)
SPLIT = 3
EXTRA = 8
VMEM_BYTES = 50 * 1024 * 1024
HIGH = lax.Precision.HIGHEST
BLOCK = 32
PANEL = 8
LANES = 128
SPARE = RANK - LANES
LOG_SCALE = math.log2(math.e) / math.sqrt(HEAD_DIM)
HIDDEN = -1e30


def params():
    return pltpu.CompilerParams(vmem_limit_bytes=VMEM_BYTES)


def vmem():
    return pl.BlockSpec(memory_space=pltpu.VMEM)


def hbm():
    return pl.BlockSpec(memory_space=pltpu.HBM)


def smem():
    return pl.BlockSpec(memory_space=pltpu.SMEM)


def nn(a, b, precision=None):
    return jnp.dot(a, b, precision=precision, preferred_element_type=jnp.float32)


def nt(a, b, precision=None):
    return lax.dot_general(
        a, b, (((1,), (1,)), ((), ())), precision=precision, preferred_element_type=jnp.float32
    )


def tn(a, b, precision=None):
    return lax.dot_general(
        a, b, (((0,), (0,)), ((), ())), precision=precision, preferred_element_type=jnp.float32
    )


def index(y, z, c):
    return (y * NZ + z) * NC + c


CORES = [[index(y, z, c) for y in range(NY) for z in range(NZ)] for c in range(NC)]


def across(x):
    pairs = [(i, i ^ 1) for i in range(NY * NZ * NC)]
    return lax.ppermute(x, "ctx", pairs)


def scatter(x):
    return lax.all_to_all(x, "ctx", 0, 0, axis_index_groups=CORES)


def gather(x):
    return scatter(jnp.broadcast_to(x, (NY * NZ, *x.shape)))


def power_kernel(
    core_ref, keys_ref, sketch_hbm, keep_ref, send_ref, keys_buf, sketch_ref, total_ref, sems, *, pieces
):
    block = keys_buf.shape[0] // pieces
    copies = []
    for i in range(pieces):
        rows = pl.ds(i * block, block)
        copies.append(
            pltpu.make_async_copy(keys_ref.at[rows, :], keys_buf.at[rows, :], sems.at[i])
        )
    copies.append(pltpu.make_async_copy(sketch_hbm, sketch_ref, sems.at[pieces]))
    for copy in (copies[pieces], *copies[:pieces]):
        copy.start()
    copies[pieces].wait()
    total, rows = None, None
    for i in range(pieces + 1):
        before = rows
        if i < pieces:
            copies[i].wait()
            keys = keys_buf[i * block : (i + 1) * block, :]
            rows = nt(keys, sketch_ref[...]).astype(jnp.bfloat16)
        if i:
            part = tn(before, keys_buf[(i - 1) * block : i * block, :])
            total = part if total is None else total + part
    total_ref[...] = total
    for at in range(KV_HEADS):
        group = jnp.bitwise_xor(core_ref[0] * HALF, at)
        lane = pl.multiple_of(group * HEAD_DIM, HEAD_DIM)
        out_ref = keep_ref if at < HALF else send_ref
        lo = at % HALF * RANK
        out_ref[lo : lo + RANK, :] = total_ref[:, pl.ds(lane, HEAD_DIM)]


def local_power(core, keys, sketch):
    positions = keys.shape[0]
    pieces = 4
    half = jax.ShapeDtypeStruct((HALF * RANK, HEAD_DIM), jnp.float32)
    return pl.pallas_call(
        lambda *refs: power_kernel(*refs, pieces=pieces),
        in_specs=[smem(), hbm(), hbm()],
        out_specs=[vmem(), vmem()],
        out_shape=[half, half],
        scratch_shapes=[
            pltpu.VMEM((positions, WIDTH), jnp.bfloat16),
            pltpu.VMEM((RANK, WIDTH), jnp.bfloat16),
            pltpu.VMEM((RANK, WIDTH), jnp.float32),
            pltpu.SemaphoreType.DMA((pieces + 1,)),
        ],
        compiler_params=params(),
    )(core, keys, sketch)


def deep(left, right, axis):
    (a, b, c), (d, e, f) = split(left, 3), split(right, 3)
    return jnp.concatenate([a, a, b, b, a, c], axis), jnp.concatenate([d, e, d, e, f, d], 0)


def eliminate(tiles, start):
    below = lax.broadcasted_iota(jnp.int32, (BLOCK, LANES), 0)
    done = []
    for panel in range(0, BLOCK, PANEL):
        at = start + panel
        own = tiles[at // LANES]
        columns = [
            jnp.broadcast_to(own[:, (at + j) % LANES : (at + j) % LANES + 1], own.shape)
            for j in range(PANEL)
        ]
        for j in range(PANEL):
            ratio = columns[j] * (1.0 / columns[j][j : j + 1])
            ratio = jnp.where(below[: BLOCK - panel] > j, ratio, 0.0)
            for m in range(j + 1, PANEL):
                columns[m] = columns[m] - ratio * columns[m][j : j + 1]
            tiles = [tile - ratio * tile[j : j + 1] for tile in tiles]
        done.append([tile[:PANEL] for tile in tiles])
        tiles = [tile[PANEL:] for tile in tiles]
    return [jnp.concatenate(pieces, axis=0) for pieces in zip(*done)]


def factor_inverse(gram, work_ref):
    row = lax.broadcasted_iota(jnp.int32, (BLOCK, LANES), 0)
    lane = lax.broadcasted_iota(jnp.int32, (BLOCK, LANES), 1)
    wide = lax.broadcasted_iota(jnp.int32, (RANK, 2 * LANES), 1)
    work_ref[...] = jnp.zeros_like(work_ref)
    work_ref[:, :RANK] = gram
    for lo in range(0, RANK, BLOCK):
        hi = lo + BLOCK
        own, offset = lo // LANES, lo % LANES
        identity = jnp.where(lane == row + SPARE, 1.0, 0.0)
        tiles = [work_ref[lo:hi, :LANES], work_ref[lo:hi, LANES:] + identity]
        tiles = eliminate(tiles, lo)
        moved = pltpu.roll(tiles[1], (offset - SPARE) % LANES, 1)
        tiles[1] = jnp.where(lane < SPARE, tiles[1], 0.0)
        diagonal = jnp.sum(jnp.where(lane == row + offset, tiles[own], 0.0), axis=1, keepdims=True)
        root = lax.rsqrt(diagonal)
        root = root * (1.5 - 0.5 * (diagonal * root) * root)
        inside = (lane >= offset) & (lane < offset + BLOCK)
        tiles[own] = jnp.where(inside, moved, tiles[own])
        rows = jnp.concatenate(tiles, axis=1) * root
        work_ref[lo:hi, :] = rows
        if hi < RANK:
            left = wide[hi:]
            rest = jnp.where((left >= lo) & (left < hi), 0.0, work_ref[hi:, :])
            work_ref[hi:, :] = rest - tn(*deep(rows[:, hi:RANK], rows, 0))
    row = lax.broadcasted_iota(jnp.int32, (RANK, 2 * LANES), 0)
    return jnp.where(wide <= row, work_ref[...], 0.0)[:, :RANK]


def split(x, count):
    out = []
    for _ in range(count):
        out.append(x.astype(jnp.bfloat16))
        x = x - out[-1].astype(jnp.float32)
    return out


def find_basis(core_ref, near_ref, far_ref, basis_ref, power_ref, work_ref):
    for at in range(KV_HEADS):
        group = jnp.bitwise_xor(core_ref[0] * HALF, at)
        lanes = pl.ds(pl.multiple_of(group * HEAD_DIM, HEAD_DIM), HEAD_DIM)
        source = near_ref if at < HALF else far_ref
        lo = at % HALF * RANK
        power_ref[:, lanes] = source[lo : lo + RANK, :]
    high, middle, low = split(power_ref[...], 3)
    cross = nt(high, middle) + nt(high, low)
    gram = nt(high, high) + (nt(middle, middle) + (cross + cross.T))
    inverse = factor_inverse(gram, work_ref)
    first, second = split(inverse, 2), (high, middle)
    left = jnp.concatenate([first[0], first[0], first[1]], axis=1)
    right = jnp.concatenate([second[0], second[1], second[0]], axis=0)
    basis_ref[...] = nn(left, right).astype(jnp.bfloat16)


def attend_kernel(
    core_ref,
    near_ref,
    far_ref,
    keys_ref,
    values_ref,
    queries_ref,
    limit_ref,
    rank_ref,
    keep_ref,
    send_ref,
    basis_ref,
    power_ref,
    work_ref,
    keys_buf,
    values_buf,
    masked_ref,
    projected_ref,
    scores_ref,
    sems,
):
    copies = [
        pltpu.make_async_copy(keys_ref, keys_buf, sems.at[0]),
        pltpu.make_async_copy(values_ref, values_buf, sems.at[1]),
        pltpu.make_async_copy(masked_ref.at[pl.ds(0, RANK), :], rank_ref, sems.at[2]),
    ]
    for copy in copies[:2]:
        copy.start()
    positions = keys_buf.shape[0]
    column = lax.broadcasted_iota(jnp.int32, (QUERIES, positions), 1)
    masked_ref[RANK:, :] = jnp.where(column < limit_ref[...], 0.0, HIDDEN).astype(jnp.bfloat16)
    row = lax.broadcasted_iota(jnp.int32, (STACKED, QUERIES), 0)
    lane = lax.broadcasted_iota(jnp.int32, (STACKED, QUERIES), 1)
    own_mask = jnp.where(row % QUERIES == lane, 1.0, 0.0).astype(jnp.bfloat16)
    find_basis(core_ref, near_ref, far_ref, basis_ref, power_ref, work_ref)
    copies[0].wait()
    for lo in range(0, positions, positions // 4):
        hi = lo + positions // 4
        rank = nt(basis_ref[...], keys_buf[lo:hi, :])
        masked_ref[:RANK, lo:hi] = rank.astype(jnp.bfloat16)
    copies[2].start()
    lane = lax.broadcasted_iota(jnp.int32, (STACKED, HEAD_DIM), 1)
    for half, out_ref in enumerate((send_ref, keep_ref)):
        start = jnp.bitwise_xor(core_ref[0], 1 - half) * HALF
        for at in range(HALF):
            g = start + at
            stacked = []
            for q in range(GROUP):
                own = pl.ds(pl.multiple_of((g * GROUP + q) * HEAD_DIM, HEAD_DIM), HEAD_DIM)
                stacked.append(queries_ref[:, own])
            stacked = jnp.concatenate(stacked, axis=0)
            lanes = pl.ds(pl.multiple_of(g * HEAD_DIM, HEAD_DIM), HEAD_DIM)
            rows = slice(at * STACKED, (at + 1) * STACKED)
            projected = nt(stacked, basis_ref[:, lanes]).astype(jnp.bfloat16)
            projected_ref[half, rows, :RANK] = projected
            projected_ref[half, rows, RANK:] = own_mask
        for lo in range(0, positions, positions // 4):
            hi = lo + positions // 4
            scores_ref[half, :, lo:hi] = nn(projected_ref[half], masked_ref[:, lo:hi])
        if half == 0:
            copies[1].wait()
        extras = jnp.zeros((STACKED, HEAD_DIM), jnp.float32)
        for pair in range(0, HALF, 2):
            weights = []
            for at in (pair, pair + 1):
                scores = scores_ref[half, at * STACKED : (at + 1) * STACKED, :]
                top = jnp.max(scores, axis=1, keepdims=True)
                expo = jnp.exp2((scores - top) * LOG_SCALE)
                total = jnp.sum(expo, axis=1, keepdims=True)
                weights.append(expo.astype(jnp.bfloat16))
                extras = jnp.where(lane == 2 * at, top * LOG_SCALE, extras)
                extras = jnp.where(lane == 2 * at + 1, total, extras)
            lanes = pl.ds(pl.multiple_of((start + pair) * HEAD_DIM, 2 * HEAD_DIM), 2 * HEAD_DIM)
            both = nn(jnp.concatenate(weights, axis=0), values_buf[:, lanes])
            out_ref[pair, :STACKED, :] = both[:STACKED, :HEAD_DIM]
            out_ref[pair + 1, :STACKED, :] = both[STACKED:, HEAD_DIM:]
        extras = extras.T
        for at in range(HALF):
            row = extras[2 * at : 2 * at + 2]
            out_ref[at, STACKED:, :] = jnp.concatenate([row] * (EXTRA // 2), axis=0)
    copies[2].wait()


def attend(core, near, far, keys, values, queries, limit):
    positions = keys.shape[0]
    return pl.pallas_call(
        attend_kernel,
        out_shape=[
            jax.ShapeDtypeStruct((RANK, positions), jnp.bfloat16),
            *[jax.ShapeDtypeStruct((HALF, STACKED + EXTRA, HEAD_DIM), jnp.float32)] * 2,
        ],
        in_specs=[smem(), vmem(), vmem(), hbm(), hbm(), vmem(), vmem()],
        out_specs=[hbm(), vmem(), vmem()],
        scratch_shapes=[
            pltpu.VMEM((RANK, WIDTH), jnp.bfloat16),
            pltpu.VMEM((RANK, WIDTH), jnp.float32),
            pltpu.VMEM((RANK, 2 * LANES), jnp.float32),
            pltpu.VMEM((positions, WIDTH), jnp.bfloat16),
            pltpu.VMEM((positions, WIDTH), jnp.bfloat16),
            pltpu.VMEM((RANK + QUERIES, positions), jnp.bfloat16),
            pltpu.VMEM((NC, HALF * STACKED, RANK + QUERIES), jnp.bfloat16),
            pltpu.VMEM((NC, HALF * STACKED, positions), jnp.float32),
            pltpu.SemaphoreType.DMA((3,)),
        ],
        compiler_params=params(),
    )(core, near, far, keys, values, queries, limit)


def columns(rows):
    pad = jnp.zeros((HEAD_DIM - rows.shape[0], rows.shape[1]), jnp.float32)
    return jnp.concatenate([rows, pad], axis=0).T


def terms(x):
    return [term.astype(jnp.float32) for term in split(x, SPLIT)]


def pair_kernel(keep_ref, sent_ref, out_ref):
    chunks = STACKED // CHUNK
    rest = jnp.zeros((EXTRA - 2 * SPLIT, STACKED), jnp.float32)
    factors, extras = [], []
    for g in range(HALF):
        tops = [ref[g, STACKED : STACKED + 1, :] for ref in (keep_ref, sent_ref)]
        totals = [ref[g, STACKED + 1 : STACKED + 2, :] for ref in (keep_ref, sent_ref)]
        top = jnp.maximum(*tops)
        pair = [jnp.exp2(t - top) for t in tops]
        total = pair[0] * totals[0] + pair[1] * totals[1]
        extras.append(jnp.concatenate([*terms(top), *terms(total), rest], axis=0))
        factors += pair
    factors = columns(jnp.concatenate(factors, axis=0))
    for g in range(HALF):
        numerator = factors[:, 2 * g : 2 * g + 1] * keep_ref[g, :STACKED]
        numerator += factors[:, 2 * g + 1 : 2 * g + 2] * sent_ref[g, :STACKED]
        for i in range(chunks):
            rows = numerator[i * CHUNK : (i + 1) * CHUNK]
            part = jnp.concatenate([rows, extras[g]], axis=0)
            out_ref[g * chunks + i] = part.astype(jnp.bfloat16)


def merge_pair(keep, sent):
    return pl.pallas_call(
        pair_kernel,
        out_shape=jax.ShapeDtypeStruct((NY * NZ, CHUNK + EXTRA, HEAD_DIM), jnp.bfloat16),
        in_specs=[vmem(), vmem()],
        out_specs=vmem(),
        compiler_params=params(),
    )(keep, sent)


def merge_kernel(at_ref, parts_ref, out_ref, factor_ref):
    count = parts_ref.shape[0]
    parts = parts_ref[...].astype(jnp.float32)
    extra = parts[:, CHUNK:, :]
    tops = sum(extra[:, i, :] for i in range(SPLIT))
    totals = sum(extra[:, SPLIT + i, :] for i in range(SPLIT))
    factors = jnp.exp2(tops - jnp.max(tops, axis=0, keepdims=True))
    total = jnp.sum(factors * totals, axis=0, keepdims=True)
    factor_ref[...] = columns(factors / total)
    own = factor_ref[pl.ds(pl.multiple_of(at_ref[0] * CHUNK, CHUNK), CHUNK), :]
    out = jnp.zeros((CHUNK, HEAD_DIM), jnp.float32)
    for i in range(count):
        out += own[:, i : i + 1] * parts[i, :CHUNK, :]
    out_ref[...] = out.astype(jnp.bfloat16)


def merge(at, parts):
    return pl.pallas_call(
        merge_kernel,
        out_shape=jax.ShapeDtypeStruct((CHUNK, HEAD_DIM), jnp.bfloat16),
        in_specs=[smem(), vmem()],
        out_specs=vmem(),
        scratch_shapes=[pltpu.VMEM((STACKED, HEAD_DIM), jnp.float32)],
        compiler_params=params(),
    )(at, parts)


def place_kernel(core_ref, near_ref, far_ref, out_ref):
    per_head = QUERIES // CHUNK
    for at in range(HEADS):
        head = jnp.bitwise_xor(core_ref[0] * (HEADS // NC), at)
        lanes = pl.ds(pl.multiple_of(head * HEAD_DIM, HEAD_DIM), HEAD_DIM)
        source = near_ref if at < HEADS // NC else far_ref
        lo = at % (HEADS // NC) * per_head
        for i in range(per_head):
            out_ref[i * CHUNK : (i + 1) * CHUNK, lanes] = source[lo + i]


def place(core, near, far):
    return pl.pallas_call(
        place_kernel,
        out_shape=jax.ShapeDtypeStruct((QUERIES, HEADS * HEAD_DIM), jnp.bfloat16),
        in_specs=[smem(), vmem(), vmem()],
        out_specs=vmem(),
        compiler_params=params(),
    )(core, near, far)


def summed(keep, send):
    part = (keep + across(send)).reshape(NY * NZ, -1, 4, HEAD_DIM)
    near = gather(jnp.sum(scatter(part), axis=0)).reshape(HALF * RANK, HEAD_DIM)
    return near, across(near)


def shards(cache_keys, cache_values, sketch_matrix, queries, visible):
    shard_rows = cache_keys.shape[0]
    me = lax.axis_index("ctx").astype(jnp.int32)
    core = (me % NC).reshape(1)
    near, far = summed(*local_power(core, cache_keys, pltpu.with_memory_space_constraint(sketch_matrix.T, pltpu.HBM)))
    limit = visible.reshape(QUERIES, 1) - me * shard_rows
    rank_keys, keep, send = attend(
        core, near, far, cache_keys, cache_values, queries.reshape(QUERIES, -1), limit
    )
    parts = scatter(merge_pair(keep, across(send)))
    chunk = merge((me // NC % (STACKED // CHUNK)).reshape(1), parts)
    near = gather(chunk)
    attended = place(core, near, across(near))
    return rank_keys.T, attended.reshape(STEPS, ROWS, HEADS * HEAD_DIM)


def solution(mesh):
    in_specs = (P("ctx", "batch"), P("ctx", "batch"), P(), P(None, "batch", None), P(None, "batch"))
    out_specs = (P("ctx", "batch"), P(None, "batch", None))
    return jax.shard_map(shards, mesh=mesh, in_specs=in_specs, out_specs=out_specs, check_vma=False)
```

```python
import math

import jax
import jax.numpy as jnp
from jax import lax
from jax.experimental import pallas as pl
from jax.experimental.pallas import tpu as pltpu
from jax.sharding import PartitionSpec as P

HEADS = 32
KV_HEADS = 8
HEAD_DIM = 128
RANK = 160
ROWS = 16
STEPS = 2
WIDTH = KV_HEADS * HEAD_DIM
GROUP = HEADS // KV_HEADS
QUERIES = STEPS * ROWS
STACKED = GROUP * QUERIES
NY = 4
NZ = 8
NC = 2
HALF = KV_HEADS // NC
CHUNK = HALF * STACKED // (NY * NZ)
SPLIT = 3
EXTRA = 8
VMEM_BYTES = 50 * 1024 * 1024
HIGH = lax.Precision.HIGHEST
BLOCK = 32
PANEL = 8
LANES = 128
SPARE = RANK - LANES
LOG_SCALE = math.log2(math.e) / math.sqrt(HEAD_DIM)
HIDDEN = -1e30


def params():
    return pltpu.CompilerParams(vmem_limit_bytes=VMEM_BYTES)


def vmem():
    return pl.BlockSpec(memory_space=pltpu.VMEM)


def hbm():
    return pl.BlockSpec(memory_space=pltpu.HBM)


def smem():
    return pl.BlockSpec(memory_space=pltpu.SMEM)


def nn(a, b, precision=None):
    return jnp.dot(a, b, precision=precision, preferred_element_type=jnp.float32)


def nt(a, b, precision=None):
    return lax.dot_general(
        a, b, (((1,), (1,)), ((), ())), precision=precision, preferred_element_type=jnp.float32
    )


def tn(a, b, precision=None):
    return lax.dot_general(
        a, b, (((0,), (0,)), ((), ())), precision=precision, preferred_element_type=jnp.float32
    )


def index(y, z, c):
    return (y * NZ + z) * NC + c


CORES = [[index(y, z, c) for y in range(NY) for z in range(NZ)] for c in range(NC)]


def across(x):
    pairs = [(i, i ^ 1) for i in range(NY * NZ * NC)]
    return lax.ppermute(x, "ctx", pairs)


def scatter(x):
    return lax.all_to_all(x, "ctx", 0, 0, axis_index_groups=CORES)


def gather(x):
    return scatter(jnp.broadcast_to(x, (NY * NZ, *x.shape)))


def power_kernel(
    core_ref, keys_ref, sketch_hbm, keep_ref, send_ref, keys_buf, sketch_ref, total_ref, sems, *, pieces
):
    block = keys_buf.shape[0] // pieces
    copies = []
    for i in range(pieces):
        rows = pl.ds(i * block, block)
        copies.append(
            pltpu.make_async_copy(keys_ref.at[rows, :], keys_buf.at[rows, :], sems.at[i])
        )
    copies.append(pltpu.make_async_copy(sketch_hbm, sketch_ref, sems.at[pieces]))
    for copy in (copies[pieces], *copies[:pieces]):
        copy.start()
    copies[pieces].wait()
    total, rows = None, None
    for i in range(pieces + 1):
        before = rows
        if i < pieces:
            copies[i].wait()
            keys = keys_buf[i * block : (i + 1) * block, :]
            rows = nt(keys, sketch_ref[...]).astype(jnp.bfloat16)
        if i:
            part = tn(before, keys_buf[(i - 1) * block : i * block, :])
            total = part if total is None else total + part
    total_ref[...] = total
    for at in range(KV_HEADS):
        group = jnp.bitwise_xor(core_ref[0] * HALF, at)
        lane = pl.multiple_of(group * HEAD_DIM, HEAD_DIM)
        out_ref = keep_ref if at < HALF else send_ref
        lo = at % HALF * RANK
        out_ref[lo : lo + RANK, :] = total_ref[:, pl.ds(lane, HEAD_DIM)]


def local_power(core, keys, sketch):
    positions = keys.shape[0]
    pieces = 4
    half = jax.ShapeDtypeStruct((HALF * RANK, HEAD_DIM), jnp.float32)
    return pl.pallas_call(
        lambda *refs: power_kernel(*refs, pieces=pieces),
        in_specs=[smem(), hbm(), hbm()],
        out_specs=[vmem(), vmem()],
        out_shape=[half, half],
        scratch_shapes=[
            pltpu.VMEM((positions, WIDTH), jnp.bfloat16),
            pltpu.VMEM((RANK, WIDTH), jnp.bfloat16),
            pltpu.VMEM((RANK, WIDTH), jnp.float32),
            pltpu.SemaphoreType.DMA((pieces + 1,)),
        ],
        compiler_params=params(),
    )(core, keys, sketch)


def deep(left, right, axis):
    (a, b, c), (d, e, f) = split(left, 3), split(right, 3)
    return jnp.concatenate([a, a, b, b, a, c], axis), jnp.concatenate([d, e, d, e, f, d], 0)


def eliminate(tiles, start):
    below = lax.broadcasted_iota(jnp.int32, (BLOCK, LANES), 0)
    done = []
    for panel in range(0, BLOCK, PANEL):
        at = start + panel
        own = tiles[at // LANES]
        columns = [
            jnp.broadcast_to(own[:, (at + j) % LANES : (at + j) % LANES + 1], own.shape)
            for j in range(PANEL)
        ]
        for j in range(PANEL):
            ratio = columns[j] * (1.0 / columns[j][j : j + 1])
            ratio = jnp.where(below[: BLOCK - panel] > j, ratio, 0.0)
            for m in range(j + 1, PANEL):
                columns[m] = columns[m] - ratio * columns[m][j : j + 1]
            tiles = [tile - ratio * tile[j : j + 1] for tile in tiles]
        done.append([tile[:PANEL] for tile in tiles])
        tiles = [tile[PANEL:] for tile in tiles]
    return [jnp.concatenate(pieces, axis=0) for pieces in zip(*done)]


def factor_inverse(gram, work_ref):
    row = lax.broadcasted_iota(jnp.int32, (BLOCK, LANES), 0)
    lane = lax.broadcasted_iota(jnp.int32, (BLOCK, LANES), 1)
    wide = lax.broadcasted_iota(jnp.int32, (RANK, 2 * LANES), 1)
    work_ref[...] = jnp.zeros_like(work_ref)
    work_ref[:, :RANK] = gram
    for lo in range(0, RANK, BLOCK):
        hi = lo + BLOCK
        own, offset = lo // LANES, lo % LANES
        identity = jnp.where(lane == row + SPARE, 1.0, 0.0)
        tiles = [work_ref[lo:hi, :LANES], work_ref[lo:hi, LANES:] + identity]
        tiles = eliminate(tiles, lo)
        moved = pltpu.roll(tiles[1], (offset - SPARE) % LANES, 1)
        tiles[1] = jnp.where(lane < SPARE, tiles[1], 0.0)
        diagonal = jnp.sum(jnp.where(lane == row + offset, tiles[own], 0.0), axis=1, keepdims=True)
        root = lax.rsqrt(diagonal)
        root = root * (1.5 - 0.5 * (diagonal * root) * root)
        inside = (lane >= offset) & (lane < offset + BLOCK)
        tiles[own] = jnp.where(inside, moved, tiles[own])
        rows = jnp.concatenate(tiles, axis=1) * root
        work_ref[lo:hi, :] = rows
        if hi < RANK:
            left = wide[hi:]
            rest = jnp.where((left >= lo) & (left < hi), 0.0, work_ref[hi:, :])
            work_ref[hi:, :] = rest - tn(*deep(rows[:, hi:RANK], rows, 0))
    row = lax.broadcasted_iota(jnp.int32, (RANK, 2 * LANES), 0)
    return jnp.where(wide <= row, work_ref[...], 0.0)[:, :RANK]


def split(x, count):
    out = []
    for _ in range(count):
        out.append(x.astype(jnp.bfloat16))
        x = x - out[-1].astype(jnp.float32)
    return out


def find_basis(core_ref, near_ref, far_ref, basis_ref, power_ref, work_ref, arrivals):
    for at in range(KV_HEADS):
        group = jnp.bitwise_xor(core_ref[0] * HALF, at)
        lanes = pl.ds(pl.multiple_of(group * HEAD_DIM, HEAD_DIM), HEAD_DIM)
        source = near_ref if at < HALF else far_ref
        lo = at % HALF * RANK
        power_ref[:, lanes] = source[lo : lo + RANK, :]
    high, middle, low = split(power_ref[...], 3)
    cross = nt(high, middle) + nt(high, low)
    gram = nt(high, high) + (nt(middle, middle) + (cross + cross.T))
    inverse = factor_inverse(gram, work_ref)
    for arrival in arrivals:
        arrival.wait()
    first, second = split(inverse, 2), (high, middle)
    left = jnp.concatenate([first[0], first[0], first[1]], axis=1)
    right = jnp.concatenate([second[0], second[1], second[0]], axis=0)
    basis_ref[...] = nn(left, right).astype(jnp.bfloat16)


def attend_kernel(
    core_ref,
    near_ref,
    far_ref,
    keys_ref,
    values_ref,
    queries_ref,
    limit_ref,
    rank_ref,
    keep_ref,
    send_ref,
    basis_ref,
    power_ref,
    work_ref,
    keys_buf,
    values_buf,
    masked_ref,
    projected_ref,
    scores_ref,
    sems,
):
    copies = [
        pltpu.make_async_copy(keys_ref, keys_buf, sems.at[0]),
        pltpu.make_async_copy(values_ref, values_buf, sems.at[1]),
        pltpu.make_async_copy(masked_ref.at[pl.ds(0, RANK), :], rank_ref, sems.at[2]),
    ]
    for copy in copies[:2]:
        copy.start()
    positions = keys_buf.shape[0]
    column = lax.broadcasted_iota(jnp.int32, (QUERIES, positions), 1)
    masked_ref[RANK:, :] = jnp.where(column < limit_ref[...], 0.0, HIDDEN).astype(jnp.bfloat16)
    row = lax.broadcasted_iota(jnp.int32, (STACKED, QUERIES), 0)
    lane = lax.broadcasted_iota(jnp.int32, (STACKED, QUERIES), 1)
    own_mask = jnp.where(row % QUERIES == lane, 1.0, 0.0).astype(jnp.bfloat16)
    for half in range(NC):
        for at in range(HALF):
            projected_ref[half, at * STACKED : (at + 1) * STACKED, RANK:] = own_mask
    find_basis(core_ref, near_ref, far_ref, basis_ref, power_ref, work_ref, copies[:2])
    starts = [jnp.bitwise_xor(core_ref[0], 1) * HALF, core_ref[0] * HALF]
    for half, start in enumerate(starts):
        for at in range(HALF):
            g = start + at
            stacked = []
            for q in range(GROUP):
                own = pl.ds(pl.multiple_of((g * GROUP + q) * HEAD_DIM, HEAD_DIM), HEAD_DIM)
                stacked.append(queries_ref[:, own])
            stacked = jnp.concatenate(stacked, axis=0)
            lanes = pl.ds(pl.multiple_of(g * HEAD_DIM, HEAD_DIM), HEAD_DIM)
            projected = nt(stacked, basis_ref[:, lanes]).astype(jnp.bfloat16)
            projected_ref[half, at * STACKED : (at + 1) * STACKED, :RANK] = projected
    block = positions // 4
    for lo in range(0, positions, block):
        rank = nt(basis_ref[...], keys_buf[lo : lo + block, :])
        masked_ref[:RANK, lo : lo + block] = rank.astype(jnp.bfloat16)

    def score(half):
        tops = None
        for lo in range(0, positions, block):
            scores = nn(projected_ref[half], masked_ref[:, lo : lo + block])
            scores_ref[half, :, lo : lo + block] = scores
            for i in range(0, block, HEAD_DIM):
                piece = scores[:, i : i + HEAD_DIM]
                tops = piece if tops is None else jnp.maximum(tops, piece)
        return jnp.max(tops, axis=1, keepdims=True)

    lane = lax.broadcasted_iota(jnp.int32, (STACKED, HEAD_DIM), 1)

    def finish(half, tops, out_ref):
        extras = jnp.zeros((STACKED, HEAD_DIM), jnp.float32)
        for pair in range(0, HALF, 2):
            weights = []
            for at in (pair, pair + 1):
                rows = slice(at * STACKED, (at + 1) * STACKED)
                expo = jnp.exp2((scores_ref[half, rows, :] - tops[rows]) * LOG_SCALE)
                total = jnp.sum(expo, axis=1, keepdims=True)
                weights.append(expo.astype(jnp.bfloat16))
                extras = jnp.where(lane == 2 * at, tops[rows] * LOG_SCALE, extras)
                extras = jnp.where(lane == 2 * at + 1, total, extras)
            first = (starts[half] + pair) * HEAD_DIM
            lanes = pl.ds(pl.multiple_of(first, 2 * HEAD_DIM), 2 * HEAD_DIM)
            both = nn(jnp.concatenate(weights, axis=0), values_buf[:, lanes])
            out_ref[pair, :STACKED, :] = both[:STACKED, :HEAD_DIM]
            out_ref[pair + 1, :STACKED, :] = both[STACKED:, HEAD_DIM:]
        extras = extras.T
        for at in range(HALF):
            row = extras[2 * at : 2 * at + 2]
            out_ref[at, STACKED:, :] = jnp.concatenate([row] * (EXTRA // 2), axis=0)

    tops = [score(half) for half in range(NC)]
    finish(0, tops[0], send_ref)
    copies[2].start()
    finish(1, tops[1], keep_ref)
    copies[2].wait()


def attend(core, near, far, keys, values, queries, limit):
    positions = keys.shape[0]
    return pl.pallas_call(
        attend_kernel,
        out_shape=[
            jax.ShapeDtypeStruct((RANK, positions), jnp.bfloat16),
            *[jax.ShapeDtypeStruct((HALF, STACKED + EXTRA, HEAD_DIM), jnp.float32)] * 2,
        ],
        in_specs=[smem(), vmem(), vmem(), hbm(), hbm(), vmem(), vmem()],
        out_specs=[hbm(), vmem(), vmem()],
        scratch_shapes=[
            pltpu.VMEM((RANK, WIDTH), jnp.bfloat16),
            pltpu.VMEM((RANK, WIDTH), jnp.float32),
            pltpu.VMEM((RANK, 2 * LANES), jnp.float32),
            pltpu.VMEM((positions, WIDTH), jnp.bfloat16),
            pltpu.VMEM((positions, WIDTH), jnp.bfloat16),
            pltpu.VMEM((RANK + QUERIES, positions), jnp.bfloat16),
            pltpu.VMEM((NC, HALF * STACKED, RANK + QUERIES), jnp.bfloat16),
            pltpu.VMEM((NC, HALF * STACKED, positions), jnp.float32),
            pltpu.SemaphoreType.DMA((3,)),
        ],
        compiler_params=params(),
    )(core, near, far, keys, values, queries, limit)


def columns(rows):
    pad = jnp.zeros((HEAD_DIM - rows.shape[0], rows.shape[1]), jnp.float32)
    return jnp.concatenate([rows, pad], axis=0).T


def terms(x):
    return [term.astype(jnp.float32) for term in split(x, SPLIT)]


def pair_kernel(keep_ref, sent_ref, out_ref):
    chunks = STACKED // CHUNK
    rest = jnp.zeros((EXTRA - 2 * SPLIT, STACKED), jnp.float32)
    factors, extras = [], []
    for g in range(HALF):
        tops = [ref[g, STACKED : STACKED + 1, :] for ref in (keep_ref, sent_ref)]
        totals = [ref[g, STACKED + 1 : STACKED + 2, :] for ref in (keep_ref, sent_ref)]
        top = jnp.maximum(*tops)
        pair = [jnp.exp2(t - top) for t in tops]
        total = pair[0] * totals[0] + pair[1] * totals[1]
        extras.append(jnp.concatenate([*terms(top), *terms(total), rest], axis=0))
        factors += pair
    factors = columns(jnp.concatenate(factors, axis=0))
    for g in range(HALF):
        numerator = factors[:, 2 * g : 2 * g + 1] * keep_ref[g, :STACKED]
        numerator += factors[:, 2 * g + 1 : 2 * g + 2] * sent_ref[g, :STACKED]
        for i in range(chunks):
            rows = numerator[i * CHUNK : (i + 1) * CHUNK]
            part = jnp.concatenate([rows, extras[g]], axis=0)
            out_ref[g * chunks + i] = part.astype(jnp.bfloat16)


def merge_pair(keep, sent):
    return pl.pallas_call(
        pair_kernel,
        out_shape=jax.ShapeDtypeStruct((NY * NZ, CHUNK + EXTRA, HEAD_DIM), jnp.bfloat16),
        in_specs=[vmem(), vmem()],
        out_specs=vmem(),
        compiler_params=params(),
    )(keep, sent)


def merge_kernel(at_ref, parts_ref, out_ref, factor_ref):
    count = parts_ref.shape[0]
    parts = parts_ref[...].astype(jnp.float32)
    extra = parts[:, CHUNK:, :]
    tops = sum(extra[:, i, :] for i in range(SPLIT))
    totals = sum(extra[:, SPLIT + i, :] for i in range(SPLIT))
    factors = jnp.exp2(tops - jnp.max(tops, axis=0, keepdims=True))
    total = jnp.sum(factors * totals, axis=0, keepdims=True)
    factor_ref[...] = columns(factors / total)
    own = factor_ref[pl.ds(pl.multiple_of(at_ref[0] * CHUNK, CHUNK), CHUNK), :]
    out = jnp.zeros((CHUNK, HEAD_DIM), jnp.float32)
    for i in range(count):
        out += own[:, i : i + 1] * parts[i, :CHUNK, :]
    out_ref[...] = out.astype(jnp.bfloat16)


def merge(at, parts):
    return pl.pallas_call(
        merge_kernel,
        out_shape=jax.ShapeDtypeStruct((CHUNK, HEAD_DIM), jnp.bfloat16),
        in_specs=[smem(), vmem()],
        out_specs=vmem(),
        scratch_shapes=[pltpu.VMEM((STACKED, HEAD_DIM), jnp.float32)],
        compiler_params=params(),
    )(at, parts)


def place_kernel(core_ref, near_ref, far_ref, out_ref):
    per_head = QUERIES // CHUNK
    for at in range(HEADS):
        head = jnp.bitwise_xor(core_ref[0] * (HEADS // NC), at)
        lanes = pl.ds(pl.multiple_of(head * HEAD_DIM, HEAD_DIM), HEAD_DIM)
        source = near_ref if at < HEADS // NC else far_ref
        lo = at % (HEADS // NC) * per_head
        for i in range(per_head):
            out_ref[i * CHUNK : (i + 1) * CHUNK, lanes] = source[lo + i]


def place(core, near, far):
    return pl.pallas_call(
        place_kernel,
        out_shape=jax.ShapeDtypeStruct((QUERIES, HEADS * HEAD_DIM), jnp.bfloat16),
        in_specs=[smem(), vmem(), vmem()],
        out_specs=vmem(),
        compiler_params=params(),
    )(core, near, far)


def summed(keep, send):
    part = (keep + across(send)).reshape(NY * NZ, -1, 4, HEAD_DIM)
    near = gather(jnp.sum(scatter(part), axis=0)).reshape(HALF * RANK, HEAD_DIM)
    return near, across(near)


def shards(cache_keys, cache_values, sketch_matrix, queries, visible):
    shard_rows = cache_keys.shape[0]
    me = lax.axis_index("ctx").astype(jnp.int32)
    core = (me % NC).reshape(1)
    near, far = summed(*local_power(core, cache_keys, pltpu.with_memory_space_constraint(sketch_matrix.T, pltpu.HBM)))
    limit = visible.reshape(QUERIES, 1) - me * shard_rows
    rank_keys, keep, send = attend(
        core, near, far, cache_keys, cache_values, queries.reshape(QUERIES, -1), limit
    )
    parts = scatter(merge_pair(keep, across(send)))
    chunk = merge((me // NC % (STACKED // CHUNK)).reshape(1), parts)
    near = gather(chunk)
    attended = place(core, near, across(near))
    return rank_keys.T, attended.reshape(STEPS, ROWS, HEADS * HEAD_DIM)


def solution(mesh):
    in_specs = (P("ctx", "batch"), P("ctx", "batch"), P(), P(None, "batch", None), P(None, "batch"))
    out_specs = (P("ctx", "batch"), P(None, "batch", None))
    return jax.shard_map(shards, mesh=mesh, in_specs=in_specs, out_specs=out_specs, check_vma=False)
```

```python
import math

import jax
import jax.numpy as jnp
from jax import lax
from jax.experimental import pallas as pl
from jax.experimental.pallas import tpu as pltpu
from jax.sharding import PartitionSpec as P

HEADS = 32
KV_HEADS = 8
HEAD_DIM = 128
RANK = 160
ROWS = 16
STEPS = 2
WIDTH = KV_HEADS * HEAD_DIM
GROUP = HEADS // KV_HEADS
QUERIES = STEPS * ROWS
STACKED = GROUP * QUERIES
NY = 4
NZ = 8
NC = 2
HALF = KV_HEADS // NC
CHUNK = HALF * STACKED // (NY * NZ)
SPLIT = 3
EXTRA = 8
VMEM_BYTES = 50 * 1024 * 1024
HIGH = lax.Precision.HIGHEST
BLOCK = 32
PANEL = 8
LANES = 128
SPARE = RANK - LANES
LOG_SCALE = math.log2(math.e) / math.sqrt(HEAD_DIM)
HIDDEN = -1e30


def params():
    return pltpu.CompilerParams(vmem_limit_bytes=VMEM_BYTES)


def vmem():
    return pl.BlockSpec(memory_space=pltpu.VMEM)


def hbm():
    return pl.BlockSpec(memory_space=pltpu.HBM)


def smem():
    return pl.BlockSpec(memory_space=pltpu.SMEM)


def nn(a, b, precision=None):
    return jnp.dot(a, b, precision=precision, preferred_element_type=jnp.float32)


def nt(a, b, precision=None):
    return lax.dot_general(
        a, b, (((1,), (1,)), ((), ())), precision=precision, preferred_element_type=jnp.float32
    )


def tn(a, b, precision=None):
    return lax.dot_general(
        a, b, (((0,), (0,)), ((), ())), precision=precision, preferred_element_type=jnp.float32
    )


def index(y, z, c):
    return (y * NZ + z) * NC + c


CORES = [[index(y, z, c) for y in range(NY) for z in range(NZ)] for c in range(NC)]


def across(x):
    pairs = [(i, i ^ 1) for i in range(NY * NZ * NC)]
    return lax.ppermute(x, "ctx", pairs)


def scatter(x):
    return lax.all_to_all(x, "ctx", 0, 0, axis_index_groups=CORES)


def gather(x):
    return scatter(jnp.broadcast_to(x, (NY * NZ, *x.shape)))


def power_kernel(
    core_ref, keys_ref, sketch_hbm, keep_ref, send_ref, keys_buf, sketch_ref, total_ref, sems, *, pieces
):
    block = keys_buf.shape[0] // pieces
    copies = []
    for i in range(pieces):
        rows = pl.ds(i * block, block)
        copies.append(
            pltpu.make_async_copy(keys_ref.at[rows, :], keys_buf.at[rows, :], sems.at[i])
        )
    copies.append(pltpu.make_async_copy(sketch_hbm, sketch_ref, sems.at[pieces]))
    for copy in (copies[pieces], *copies[:pieces]):
        copy.start()
    copies[pieces].wait()
    total, rows = None, None
    for i in range(pieces + 1):
        before = rows
        if i < pieces:
            copies[i].wait()
            keys = keys_buf[i * block : (i + 1) * block, :]
            rows = nt(keys, sketch_ref[...]).astype(jnp.bfloat16)
        if i:
            part = tn(before, keys_buf[(i - 1) * block : i * block, :])
            total = part if total is None else total + part
    total_ref[...] = total
    for at in range(KV_HEADS):
        group = jnp.bitwise_xor(core_ref[0] * HALF, at)
        lane = pl.multiple_of(group * HEAD_DIM, HEAD_DIM)
        out_ref = keep_ref if at < HALF else send_ref
        lo = at % HALF * RANK
        out_ref[lo : lo + RANK, :] = total_ref[:, pl.ds(lane, HEAD_DIM)]


def local_power(core, keys, sketch):
    positions = keys.shape[0]
    pieces = 4
    half = jax.ShapeDtypeStruct((HALF * RANK, HEAD_DIM), jnp.float32)
    return pl.pallas_call(
        lambda *refs: power_kernel(*refs, pieces=pieces),
        in_specs=[smem(), hbm(), hbm()],
        out_specs=[vmem(), vmem()],
        out_shape=[half, half],
        scratch_shapes=[
            pltpu.VMEM((positions, WIDTH), jnp.bfloat16),
            pltpu.VMEM((RANK, WIDTH), jnp.bfloat16),
            pltpu.VMEM((RANK, WIDTH), jnp.float32),
            pltpu.SemaphoreType.DMA((pieces + 1,)),
        ],
        compiler_params=params(),
    )(core, keys, sketch)


def deep(left, right, axis):
    (a, b, c), (d, e, f) = split(left, 3), split(right, 3)
    return jnp.concatenate([a, a, b, b, a, c], axis), jnp.concatenate([d, e, d, e, f, d], 0)


def eliminate(tiles, start):
    below = lax.broadcasted_iota(jnp.int32, (BLOCK, LANES), 0)
    done = []
    for panel in range(0, BLOCK, PANEL):
        at = start + panel
        own = tiles[at // LANES]
        columns = [
            jnp.broadcast_to(own[:, (at + j) % LANES : (at + j) % LANES + 1], own.shape)
            for j in range(PANEL)
        ]
        for j in range(PANEL):
            ratio = columns[j] * (1.0 / columns[j][j : j + 1])
            ratio = jnp.where(below[: BLOCK - panel] > j, ratio, 0.0)
            for m in range(j + 1, PANEL):
                columns[m] = columns[m] - ratio * columns[m][j : j + 1]
            tiles = [tile - ratio * tile[j : j + 1] for tile in tiles]
        done.append([tile[:PANEL] for tile in tiles])
        tiles = [tile[PANEL:] for tile in tiles]
    return [jnp.concatenate(pieces, axis=0) for pieces in zip(*done)]


def factor_inverse(gram, work_ref):
    row = lax.broadcasted_iota(jnp.int32, (BLOCK, LANES), 0)
    lane = lax.broadcasted_iota(jnp.int32, (BLOCK, LANES), 1)
    wide = lax.broadcasted_iota(jnp.int32, (RANK, 2 * LANES), 1)
    work_ref[...] = jnp.zeros_like(work_ref)
    work_ref[:, :RANK] = gram
    for lo in range(0, RANK, BLOCK):
        hi = lo + BLOCK
        own, offset = lo // LANES, lo % LANES
        identity = jnp.where(lane == row + SPARE, 1.0, 0.0)
        tiles = [work_ref[lo:hi, :LANES], work_ref[lo:hi, LANES:] + identity]
        tiles = eliminate(tiles, lo)
        moved = pltpu.roll(tiles[1], (offset - SPARE) % LANES, 1)
        tiles[1] = jnp.where(lane < SPARE, tiles[1], 0.0)
        diagonal = jnp.sum(jnp.where(lane == row + offset, tiles[own], 0.0), axis=1, keepdims=True)
        root = lax.rsqrt(diagonal)
        root = root * (1.5 - 0.5 * (diagonal * root) * root)
        inside = (lane >= offset) & (lane < offset + BLOCK)
        tiles[own] = jnp.where(inside, moved, tiles[own])
        rows = jnp.concatenate(tiles, axis=1) * root
        work_ref[lo:hi, :] = rows
        if hi < RANK:
            left = wide[hi:]
            rest = jnp.where((left >= lo) & (left < hi), 0.0, work_ref[hi:, :])
            work_ref[hi:, :] = rest - tn(*deep(rows[:, hi:RANK], rows, 0))
    row = lax.broadcasted_iota(jnp.int32, (RANK, 2 * LANES), 0)
    return jnp.where(wide <= row, work_ref[...], 0.0)[:, :RANK]


def split(x, count):
    out = []
    for _ in range(count):
        out.append(x.astype(jnp.bfloat16))
        x = x - out[-1].astype(jnp.float32)
    return out


def find_basis(core_ref, near_ref, far_ref, basis_ref, power_ref, work_ref):
    for at in range(KV_HEADS):
        group = jnp.bitwise_xor(core_ref[0] * HALF, at)
        lanes = pl.ds(pl.multiple_of(group * HEAD_DIM, HEAD_DIM), HEAD_DIM)
        source = near_ref if at < HALF else far_ref
        lo = at % HALF * RANK
        power_ref[:, lanes] = source[lo : lo + RANK, :]
    high, middle, low = split(power_ref[...], 3)
    cross = nt(high, middle) + nt(high, low)
    gram = nt(high, high) + (nt(middle, middle) + (cross + cross.T))
    inverse = factor_inverse(gram, work_ref)
    first, second = split(inverse, 2), (high, middle)
    left = jnp.concatenate([first[0], first[0], first[1]], axis=1)
    right = jnp.concatenate([second[0], second[1], second[0]], axis=0)
    basis_ref[...] = nn(left, right).astype(jnp.bfloat16)


def attend_kernel(
    core_ref,
    near_ref,
    far_ref,
    keys_ref,
    values_ref,
    queries_ref,
    limit_ref,
    rank_ref,
    keep_ref,
    send_ref,
    basis_ref,
    power_ref,
    work_ref,
    keys_buf,
    values_buf,
    masked_ref,
    projected_ref,
    scores_ref,
    weights_ref,
    sems,
):
    copies = [
        pltpu.make_async_copy(keys_ref, keys_buf, sems.at[0]),
        pltpu.make_async_copy(values_ref, values_buf, sems.at[1]),
        pltpu.make_async_copy(masked_ref.at[pl.ds(0, RANK), :], rank_ref, sems.at[2]),
    ]
    for copy in copies[:2]:
        copy.start()
    positions = keys_buf.shape[0]
    column = lax.broadcasted_iota(jnp.int32, (QUERIES, positions), 1)
    masked_ref[RANK:, :] = jnp.where(column < limit_ref[...], 0.0, HIDDEN).astype(jnp.bfloat16)
    row = lax.broadcasted_iota(jnp.int32, (STACKED, QUERIES), 0)
    lane = lax.broadcasted_iota(jnp.int32, (STACKED, QUERIES), 1)
    own_mask = jnp.where(row % QUERIES == lane, 1.0, 0.0).astype(jnp.bfloat16)
    find_basis(core_ref, near_ref, far_ref, basis_ref, power_ref, work_ref)
    copies[0].wait()
    for lo in range(0, positions, positions // 4):
        hi = lo + positions // 4
        rank = nt(basis_ref[...], keys_buf[lo:hi, :])
        masked_ref[:RANK, lo:hi] = rank.astype(jnp.bfloat16)
    copies[2].start()
    lane = lax.broadcasted_iota(jnp.int32, (STACKED, HEAD_DIM), 1)
    for half, out_ref in enumerate((send_ref, keep_ref)):
        start = jnp.bitwise_xor(core_ref[0], 1 - half) * HALF
        for at in range(HALF):
            g = start + at
            stacked = []
            for q in range(GROUP):
                own = pl.ds(pl.multiple_of((g * GROUP + q) * HEAD_DIM, HEAD_DIM), HEAD_DIM)
                stacked.append(queries_ref[:, own])
            stacked = jnp.concatenate(stacked, axis=0)
            lanes = pl.ds(pl.multiple_of(g * HEAD_DIM, HEAD_DIM), HEAD_DIM)
            rows = slice(at * STACKED, (at + 1) * STACKED)
            projected = nt(stacked, basis_ref[:, lanes]).astype(jnp.bfloat16)
            projected_ref[half, rows, :RANK] = projected
            projected_ref[half, rows, RANK:] = own_mask
        for lo in range(0, positions, positions // 4):
            hi = lo + positions // 4
            scores_ref[half, :, lo:hi] = nn(projected_ref[half], masked_ref[:, lo:hi])
        if half == 0:
            copies[1].wait()
        extras = jnp.zeros((STACKED, HEAD_DIM), jnp.float32)
        for pair in range(0, HALF, 2):
            for at in (pair, pair + 1):
                rows = slice(at * STACKED, (at + 1) * STACKED)
                tops = None
                for lo in range(0, positions, LANES):
                    piece = scores_ref[half, rows, lo : lo + LANES]
                    tops = piece if tops is None else jnp.maximum(tops, piece)
                top = jnp.max(tops, axis=1, keepdims=True)
                totals = None
                for lo in range(0, positions, LANES):
                    piece = scores_ref[half, rows, lo : lo + LANES]
                    expo = jnp.exp2((piece - top) * LOG_SCALE)
                    totals = expo if totals is None else totals + expo
                    weights_ref[half, rows, lo : lo + LANES] = expo.astype(jnp.bfloat16)
                total = jnp.sum(totals, axis=1, keepdims=True)
                extras = jnp.where(lane == 2 * at, top * LOG_SCALE, extras)
                extras = jnp.where(lane == 2 * at + 1, total, extras)
            lanes = pl.ds(pl.multiple_of((start + pair) * HEAD_DIM, 2 * HEAD_DIM), 2 * HEAD_DIM)
            rows = slice(pair * STACKED, (pair + 2) * STACKED)
            both = nn(weights_ref[half, rows, :], values_buf[:, lanes])
            out_ref[pair, :STACKED, :] = both[:STACKED, :HEAD_DIM]
            out_ref[pair + 1, :STACKED, :] = both[STACKED:, HEAD_DIM:]
        extras = extras.T
        for at in range(HALF):
            row = extras[2 * at : 2 * at + 2]
            out_ref[at, STACKED:, :] = jnp.concatenate([row] * (EXTRA // 2), axis=0)
    copies[2].wait()


def attend(core, near, far, keys, values, queries, limit):
    positions = keys.shape[0]
    return pl.pallas_call(
        attend_kernel,
        out_shape=[
            jax.ShapeDtypeStruct((RANK, positions), jnp.bfloat16),
            *[jax.ShapeDtypeStruct((HALF, STACKED + EXTRA, HEAD_DIM), jnp.float32)] * 2,
        ],
        in_specs=[smem(), vmem(), vmem(), hbm(), hbm(), vmem(), vmem()],
        out_specs=[hbm(), vmem(), vmem()],
        scratch_shapes=[
            pltpu.VMEM((RANK, WIDTH), jnp.bfloat16),
            pltpu.VMEM((RANK, WIDTH), jnp.float32),
            pltpu.VMEM((RANK, 2 * LANES), jnp.float32),
            pltpu.VMEM((positions, WIDTH), jnp.bfloat16),
            pltpu.VMEM((positions, WIDTH), jnp.bfloat16),
            pltpu.VMEM((RANK + QUERIES, positions), jnp.bfloat16),
            pltpu.VMEM((NC, HALF * STACKED, RANK + QUERIES), jnp.bfloat16),
            pltpu.VMEM((NC, HALF * STACKED, positions), jnp.float32),
            pltpu.VMEM((NC, HALF * STACKED, positions), jnp.bfloat16),
            pltpu.SemaphoreType.DMA((3,)),
        ],
        compiler_params=params(),
    )(core, near, far, keys, values, queries, limit)


def columns(rows):
    pad = jnp.zeros((HEAD_DIM - rows.shape[0], rows.shape[1]), jnp.float32)
    return jnp.concatenate([rows, pad], axis=0).T


def terms(x):
    return [term.astype(jnp.float32) for term in split(x, SPLIT)]


def pair_kernel(keep_ref, sent_ref, out_ref):
    chunks = STACKED // CHUNK
    rest = jnp.zeros((EXTRA - 2 * SPLIT, STACKED), jnp.float32)
    factors, extras = [], []
    for g in range(HALF):
        tops = [ref[g, STACKED : STACKED + 1, :] for ref in (keep_ref, sent_ref)]
        totals = [ref[g, STACKED + 1 : STACKED + 2, :] for ref in (keep_ref, sent_ref)]
        top = jnp.maximum(*tops)
        pair = [jnp.exp2(t - top) for t in tops]
        total = pair[0] * totals[0] + pair[1] * totals[1]
        extras.append(jnp.concatenate([*terms(top), *terms(total), rest], axis=0))
        factors += pair
    factors = columns(jnp.concatenate(factors, axis=0))
    for g in range(HALF):
        numerator = factors[:, 2 * g : 2 * g + 1] * keep_ref[g, :STACKED]
        numerator += factors[:, 2 * g + 1 : 2 * g + 2] * sent_ref[g, :STACKED]
        for i in range(chunks):
            rows = numerator[i * CHUNK : (i + 1) * CHUNK]
            part = jnp.concatenate([rows, extras[g]], axis=0)
            out_ref[g * chunks + i] = part.astype(jnp.bfloat16)


def merge_pair(keep, sent):
    return pl.pallas_call(
        pair_kernel,
        out_shape=jax.ShapeDtypeStruct((NY * NZ, CHUNK + EXTRA, HEAD_DIM), jnp.bfloat16),
        in_specs=[vmem(), vmem()],
        out_specs=vmem(),
        compiler_params=params(),
    )(keep, sent)


def merge_kernel(at_ref, parts_ref, out_ref, factor_ref):
    count = parts_ref.shape[0]
    parts = parts_ref[...].astype(jnp.float32)
    extra = parts[:, CHUNK:, :]
    tops = sum(extra[:, i, :] for i in range(SPLIT))
    totals = sum(extra[:, SPLIT + i, :] for i in range(SPLIT))
    factors = jnp.exp2(tops - jnp.max(tops, axis=0, keepdims=True))
    total = jnp.sum(factors * totals, axis=0, keepdims=True)
    factor_ref[...] = columns(factors / total)
    own = factor_ref[pl.ds(pl.multiple_of(at_ref[0] * CHUNK, CHUNK), CHUNK), :]
    out = jnp.zeros((CHUNK, HEAD_DIM), jnp.float32)
    for i in range(count):
        out += own[:, i : i + 1] * parts[i, :CHUNK, :]
    out_ref[...] = out.astype(jnp.bfloat16)


def merge(at, parts):
    return pl.pallas_call(
        merge_kernel,
        out_shape=jax.ShapeDtypeStruct((CHUNK, HEAD_DIM), jnp.bfloat16),
        in_specs=[smem(), vmem()],
        out_specs=vmem(),
        scratch_shapes=[pltpu.VMEM((STACKED, HEAD_DIM), jnp.float32)],
        compiler_params=params(),
    )(at, parts)


def place_kernel(core_ref, near_ref, far_ref, out_ref):
    per_head = QUERIES // CHUNK
    for at in range(HEADS):
        head = jnp.bitwise_xor(core_ref[0] * (HEADS // NC), at)
        lanes = pl.ds(pl.multiple_of(head * HEAD_DIM, HEAD_DIM), HEAD_DIM)
        source = near_ref if at < HEADS // NC else far_ref
        lo = at % (HEADS // NC) * per_head
        for i in range(per_head):
            out_ref[i * CHUNK : (i + 1) * CHUNK, lanes] = source[lo + i]


def place(core, near, far):
    return pl.pallas_call(
        place_kernel,
        out_shape=jax.ShapeDtypeStruct((QUERIES, HEADS * HEAD_DIM), jnp.bfloat16),
        in_specs=[smem(), vmem(), vmem()],
        out_specs=vmem(),
        compiler_params=params(),
    )(core, near, far)


def summed(keep, send):
    part = (keep + across(send)).reshape(NY * NZ, -1, 4, HEAD_DIM)
    near = gather(jnp.sum(scatter(part), axis=0)).reshape(HALF * RANK, HEAD_DIM)
    return near, across(near)


def shards(cache_keys, cache_values, sketch_matrix, queries, visible):
    shard_rows = cache_keys.shape[0]
    me = lax.axis_index("ctx").astype(jnp.int32)
    core = (me % NC).reshape(1)
    near, far = summed(*local_power(core, cache_keys, pltpu.with_memory_space_constraint(sketch_matrix.T, pltpu.HBM)))
    limit = visible.reshape(QUERIES, 1) - me * shard_rows
    rank_keys, keep, send = attend(
        core, near, far, cache_keys, cache_values, queries.reshape(QUERIES, -1), limit
    )
    parts = scatter(merge_pair(keep, across(send)))
    chunk = merge((me // NC % (STACKED // CHUNK)).reshape(1), parts)
    near = gather(chunk)
    attended = place(core, near, across(near))
    return rank_keys.T, attended.reshape(STEPS, ROWS, HEADS * HEAD_DIM)


def solution(mesh):
    in_specs = (P("ctx", "batch"), P("ctx", "batch"), P(), P(None, "batch", None), P(None, "batch"))
    out_specs = (P("ctx", "batch"), P(None, "batch", None))
    return jax.shard_map(shards, mesh=mesh, in_specs=in_specs, out_specs=out_specs, check_vma=False)
```

```python
import math

import jax
import jax.numpy as jnp
from jax import lax
from jax.experimental import pallas as pl
from jax.experimental.pallas import tpu as pltpu
from jax.sharding import PartitionSpec as P

HEADS = 32
KV_HEADS = 8
HEAD_DIM = 128
RANK = 160
ROWS = 16
STEPS = 2
WIDTH = KV_HEADS * HEAD_DIM
GROUP = HEADS // KV_HEADS
QUERIES = STEPS * ROWS
STACKED = GROUP * QUERIES
NY = 4
NZ = 8
NC = 2
HALF = KV_HEADS // NC
CHUNK = HALF * STACKED // (NY * NZ)
SPLIT = 3
EXTRA = 8
VMEM_BYTES = 50 * 1024 * 1024
HIGH = lax.Precision.HIGHEST
BLOCK = 32
PANEL = 8
LANES = 128
SPARE = RANK - LANES
LOG_SCALE = math.log2(math.e) / math.sqrt(HEAD_DIM)
HIDDEN = -1e30


def params():
    return pltpu.CompilerParams(vmem_limit_bytes=VMEM_BYTES)


def vmem():
    return pl.BlockSpec(memory_space=pltpu.VMEM)


def hbm():
    return pl.BlockSpec(memory_space=pltpu.HBM)


def smem():
    return pl.BlockSpec(memory_space=pltpu.SMEM)


def nn(a, b, precision=None):
    return jnp.dot(a, b, precision=precision, preferred_element_type=jnp.float32)


def nt(a, b, precision=None):
    return lax.dot_general(
        a, b, (((1,), (1,)), ((), ())), precision=precision, preferred_element_type=jnp.float32
    )


def tn(a, b, precision=None):
    return lax.dot_general(
        a, b, (((0,), (0,)), ((), ())), precision=precision, preferred_element_type=jnp.float32
    )


def index(y, z, c):
    return (y * NZ + z) * NC + c


CORES = [[index(y, z, c) for y in range(NY) for z in range(NZ)] for c in range(NC)]


def across(x):
    pairs = [(i, i ^ 1) for i in range(NY * NZ * NC)]
    return lax.ppermute(x, "ctx", pairs)


def scatter(x):
    return lax.all_to_all(x, "ctx", 0, 0, axis_index_groups=CORES)


def gather(x):
    return scatter(jnp.broadcast_to(x, (NY * NZ, *x.shape)))


def power_kernel(
    core_ref, keys_ref, sketch_hbm, keep_ref, send_ref, keys_buf, sketch_ref, total_ref, sems, *, pieces
):
    block = keys_buf.shape[0] // pieces
    copies = []
    for i in range(pieces):
        rows = pl.ds(i * block, block)
        copies.append(
            pltpu.make_async_copy(keys_ref.at[rows, :], keys_buf.at[rows, :], sems.at[i])
        )
    copies.append(pltpu.make_async_copy(sketch_hbm, sketch_ref, sems.at[pieces]))
    for copy in (copies[pieces], *copies[:pieces]):
        copy.start()
    copies[pieces].wait()
    total, rows = None, None
    for i in range(pieces + 1):
        before = rows
        if i < pieces:
            copies[i].wait()
            keys = keys_buf[i * block : (i + 1) * block, :]
            rows = nt(keys, sketch_ref[...]).astype(jnp.bfloat16)
        if i:
            part = tn(before, keys_buf[(i - 1) * block : i * block, :])
            total = part if total is None else total + part
    total_ref[...] = total
    for at in range(KV_HEADS):
        group = jnp.bitwise_xor(core_ref[0] * HALF, at)
        lane = pl.multiple_of(group * HEAD_DIM, HEAD_DIM)
        out_ref = keep_ref if at < HALF else send_ref
        lo = at % HALF * RANK
        out_ref[lo : lo + RANK, :] = total_ref[:, pl.ds(lane, HEAD_DIM)]


def local_power(core, keys, sketch):
    positions = keys.shape[0]
    pieces = 4
    half = jax.ShapeDtypeStruct((HALF * RANK, HEAD_DIM), jnp.float32)
    return pl.pallas_call(
        lambda *refs: power_kernel(*refs, pieces=pieces),
        in_specs=[smem(), hbm(), hbm()],
        out_specs=[vmem(), vmem()],
        out_shape=[half, half],
        scratch_shapes=[
            pltpu.VMEM((positions, WIDTH), jnp.bfloat16),
            pltpu.VMEM((RANK, WIDTH), jnp.bfloat16),
            pltpu.VMEM((RANK, WIDTH), jnp.float32),
            pltpu.SemaphoreType.DMA((pieces + 1,)),
        ],
        compiler_params=params(),
    )(core, keys, sketch)


def deep(left, right, axis):
    (a, b, c), (d, e, f) = split(left, 3), split(right, 3)
    return jnp.concatenate([a, a, b, b, a, c], axis), jnp.concatenate([d, e, d, e, f, d], 0)


def eliminate(tiles, start):
    below = lax.broadcasted_iota(jnp.int32, (BLOCK, LANES), 0)
    done = []
    for panel in range(0, BLOCK, PANEL):
        at = start + panel
        own = tiles[at // LANES]
        columns = [
            jnp.broadcast_to(own[:, (at + j) % LANES : (at + j) % LANES + 1], own.shape)
            for j in range(PANEL)
        ]
        for j in range(PANEL):
            ratio = columns[j] * (1.0 / columns[j][j : j + 1])
            top = jnp.where(below[:PANEL] > j, ratio[:PANEL], 0.0)
            ratio = jnp.concatenate([top, ratio[PANEL:]], axis=0) if panel + PANEL < BLOCK else top
            for m in range(j + 1, PANEL):
                columns[m] = columns[m] - ratio * columns[m][j : j + 1]
            tiles = [tile - ratio * tile[j : j + 1] for tile in tiles]
        done.append([tile[:PANEL] for tile in tiles])
        tiles = [tile[PANEL:] for tile in tiles]
    return [jnp.concatenate(pieces, axis=0) for pieces in zip(*done)]


def factor_inverse(gram, work_ref):
    row = lax.broadcasted_iota(jnp.int32, (BLOCK, LANES), 0)
    lane = lax.broadcasted_iota(jnp.int32, (BLOCK, LANES), 1)
    wide = lax.broadcasted_iota(jnp.int32, (RANK, 2 * LANES), 1)
    work_ref[...] = jnp.zeros_like(work_ref)
    work_ref[:, :RANK] = gram
    for lo in range(0, RANK, BLOCK):
        hi = lo + BLOCK
        own, offset = lo // LANES, lo % LANES
        identity = jnp.where(lane == row + SPARE, 1.0, 0.0)
        tiles = [work_ref[lo:hi, :LANES], work_ref[lo:hi, LANES:] + identity]
        tiles = eliminate(tiles, lo)
        moved = pltpu.roll(tiles[1], (offset - SPARE) % LANES, 1)
        tiles[1] = jnp.where(lane < SPARE, tiles[1], 0.0)
        diagonal = jnp.sum(jnp.where(lane == row + offset, tiles[own], 0.0), axis=1, keepdims=True)
        root = lax.rsqrt(diagonal)
        root = root * (1.5 - 0.5 * (diagonal * root) * root)
        inside = (lane >= offset) & (lane < offset + BLOCK)
        tiles[own] = jnp.where(inside, moved, tiles[own])
        rows = jnp.concatenate(tiles, axis=1) * root
        work_ref[lo:hi, :] = rows
        if hi < RANK:
            left = wide[hi:]
            rest = jnp.where((left >= lo) & (left < hi), 0.0, work_ref[hi:, :])
            work_ref[hi:, :] = rest - tn(*deep(rows[:, hi:RANK], rows, 0))
    row = lax.broadcasted_iota(jnp.int32, (RANK, 2 * LANES), 0)
    return jnp.where(wide <= row, work_ref[...], 0.0)[:, :RANK]


def split(x, count):
    out = []
    for _ in range(count):
        out.append(x.astype(jnp.bfloat16))
        x = x - out[-1].astype(jnp.float32)
    return out


def find_basis(core_ref, near_ref, far_ref, basis_ref, power_ref, work_ref, arrivals):
    for at in range(KV_HEADS):
        group = jnp.bitwise_xor(core_ref[0] * HALF, at)
        lanes = pl.ds(pl.multiple_of(group * HEAD_DIM, HEAD_DIM), HEAD_DIM)
        source = near_ref if at < HALF else far_ref
        lo = at % HALF * RANK
        power_ref[:, lanes] = source[lo : lo + RANK, :]
    high, middle, low = split(power_ref[...], 3)
    cross = nt(high, middle) + nt(high, low)
    gram = nt(high, high) + (nt(middle, middle) + (cross + cross.T))
    inverse = factor_inverse(gram, work_ref)
    for arrival in arrivals:
        arrival.wait()
    first, second = split(inverse, 2), (high, middle)
    left = jnp.concatenate([first[0], first[0], first[1]], axis=1)
    right = jnp.concatenate([second[0], second[1], second[0]], axis=0)
    basis_ref[...] = nn(left, right).astype(jnp.bfloat16)


def attend_kernel(
    core_ref,
    near_ref,
    far_ref,
    keys_ref,
    values_ref,
    queries_ref,
    limit_ref,
    rank_ref,
    keep_ref,
    send_ref,
    basis_ref,
    power_ref,
    work_ref,
    keys_buf,
    values_buf,
    masked_ref,
    projected_ref,
    scores_ref,
    sems,
):
    copies = [
        pltpu.make_async_copy(keys_ref, keys_buf, sems.at[0]),
        pltpu.make_async_copy(values_ref, values_buf, sems.at[1]),
        pltpu.make_async_copy(masked_ref.at[pl.ds(0, RANK), :], rank_ref, sems.at[2]),
    ]
    for copy in copies[:2]:
        copy.start()
    positions = keys_buf.shape[0]
    column = lax.broadcasted_iota(jnp.int32, (QUERIES, positions), 1)
    masked_ref[RANK:, :] = jnp.where(column < limit_ref[...], 0.0, HIDDEN).astype(jnp.bfloat16)
    row = lax.broadcasted_iota(jnp.int32, (STACKED, QUERIES), 0)
    lane = lax.broadcasted_iota(jnp.int32, (STACKED, QUERIES), 1)
    own_mask = jnp.where(row % QUERIES == lane, 1.0, 0.0).astype(jnp.bfloat16)
    find_basis(core_ref, near_ref, far_ref, basis_ref, power_ref, work_ref, copies[:2])
    for lo in range(0, positions, positions // 4):
        hi = lo + positions // 4
        rank = nt(basis_ref[...], keys_buf[lo:hi, :])
        masked_ref[:RANK, lo:hi] = rank.astype(jnp.bfloat16)
    copies[2].start()
    lane = lax.broadcasted_iota(jnp.int32, (STACKED, HEAD_DIM), 1)
    for half, out_ref in enumerate((send_ref, keep_ref)):
        start = jnp.bitwise_xor(core_ref[0], 1 - half) * HALF
        for at in range(HALF):
            g = start + at
            stacked = []
            for q in range(GROUP):
                own = pl.ds(pl.multiple_of((g * GROUP + q) * HEAD_DIM, HEAD_DIM), HEAD_DIM)
                stacked.append(queries_ref[:, own])
            stacked = jnp.concatenate(stacked, axis=0)
            lanes = pl.ds(pl.multiple_of(g * HEAD_DIM, HEAD_DIM), HEAD_DIM)
            rows = slice(at * STACKED, (at + 1) * STACKED)
            projected = nt(stacked, basis_ref[:, lanes]).astype(jnp.bfloat16)
            projected_ref[half, rows, :RANK] = projected
            projected_ref[half, rows, RANK:] = own_mask
        for lo in range(0, positions, positions // 4):
            hi = lo + positions // 4
            scores_ref[half, :, lo:hi] = nn(projected_ref[half], masked_ref[:, lo:hi])
        extras = jnp.zeros((STACKED, HEAD_DIM), jnp.float32)
        for pair in range(0, HALF, 2):
            weights = []
            for at in (pair, pair + 1):
                scores = scores_ref[half, at * STACKED : (at + 1) * STACKED, :]
                top = jnp.max(scores, axis=1, keepdims=True)
                expo = jnp.exp2((scores - top) * LOG_SCALE)
                total = jnp.sum(expo, axis=1, keepdims=True)
                weights.append(expo.astype(jnp.bfloat16))
                extras = jnp.where(lane == 2 * at, top * LOG_SCALE, extras)
                extras = jnp.where(lane == 2 * at + 1, total, extras)
            lanes = pl.ds(pl.multiple_of((start + pair) * HEAD_DIM, 2 * HEAD_DIM), 2 * HEAD_DIM)
            both = nn(jnp.concatenate(weights, axis=0), values_buf[:, lanes])
            out_ref[pair, :STACKED, :] = both[:STACKED, :HEAD_DIM]
            out_ref[pair + 1, :STACKED, :] = both[STACKED:, HEAD_DIM:]
        extras = extras.T
        for at in range(HALF):
            row = extras[2 * at : 2 * at + 2]
            out_ref[at, STACKED:, :] = jnp.concatenate([row] * (EXTRA // 2), axis=0)
    copies[2].wait()


def attend(core, near, far, keys, values, queries, limit):
    positions = keys.shape[0]
    return pl.pallas_call(
        attend_kernel,
        out_shape=[
            jax.ShapeDtypeStruct((RANK, positions), jnp.bfloat16),
            *[jax.ShapeDtypeStruct((HALF, STACKED + EXTRA, HEAD_DIM), jnp.float32)] * 2,
        ],
        in_specs=[smem(), vmem(), vmem(), hbm(), hbm(), vmem(), vmem()],
        out_specs=[hbm(), vmem(), vmem()],
        scratch_shapes=[
            pltpu.VMEM((RANK, WIDTH), jnp.bfloat16),
            pltpu.VMEM((RANK, WIDTH), jnp.float32),
            pltpu.VMEM((RANK, 2 * LANES), jnp.float32),
            pltpu.VMEM((positions, WIDTH), jnp.bfloat16),
            pltpu.VMEM((positions, WIDTH), jnp.bfloat16),
            pltpu.VMEM((RANK + QUERIES, positions), jnp.bfloat16),
            pltpu.VMEM((NC, HALF * STACKED, RANK + QUERIES), jnp.bfloat16),
            pltpu.VMEM((NC, HALF * STACKED, positions), jnp.float32),
            pltpu.SemaphoreType.DMA((3,)),
        ],
        compiler_params=params(),
    )(core, near, far, keys, values, queries, limit)


def columns(rows):
    pad = jnp.zeros((HEAD_DIM - rows.shape[0], rows.shape[1]), jnp.float32)
    return jnp.concatenate([rows, pad], axis=0).T


def terms(x):
    return [term.astype(jnp.float32) for term in split(x, SPLIT)]


def pair_kernel(keep_ref, sent_ref, out_ref):
    chunks = STACKED // CHUNK
    rest = jnp.zeros((EXTRA - 2 * SPLIT, STACKED), jnp.float32)
    factors, extras = [], []
    for g in range(HALF):
        tops = [ref[g, STACKED : STACKED + 1, :] for ref in (keep_ref, sent_ref)]
        totals = [ref[g, STACKED + 1 : STACKED + 2, :] for ref in (keep_ref, sent_ref)]
        top = jnp.maximum(*tops)
        pair = [jnp.exp2(t - top) for t in tops]
        total = pair[0] * totals[0] + pair[1] * totals[1]
        extras.append(jnp.concatenate([*terms(top), *terms(total), rest], axis=0))
        factors += pair
    factors = columns(jnp.concatenate(factors, axis=0))
    for g in range(HALF):
        numerator = factors[:, 2 * g : 2 * g + 1] * keep_ref[g, :STACKED]
        numerator += factors[:, 2 * g + 1 : 2 * g + 2] * sent_ref[g, :STACKED]
        for i in range(chunks):
            rows = numerator[i * CHUNK : (i + 1) * CHUNK]
            part = jnp.concatenate([rows, extras[g]], axis=0)
            out_ref[g * chunks + i] = part.astype(jnp.bfloat16)


def merge_pair(keep, sent):
    return pl.pallas_call(
        pair_kernel,
        out_shape=jax.ShapeDtypeStruct((NY * NZ, CHUNK + EXTRA, HEAD_DIM), jnp.bfloat16),
        in_specs=[vmem(), vmem()],
        out_specs=vmem(),
        compiler_params=params(),
    )(keep, sent)


def merge_kernel(at_ref, parts_ref, out_ref, factor_ref):
    count = parts_ref.shape[0]
    parts = parts_ref[...].astype(jnp.float32)
    extra = parts[:, CHUNK:, :]
    tops = sum(extra[:, i, :] for i in range(SPLIT))
    totals = sum(extra[:, SPLIT + i, :] for i in range(SPLIT))
    factors = jnp.exp2(tops - jnp.max(tops, axis=0, keepdims=True))
    total = jnp.sum(factors * totals, axis=0, keepdims=True)
    factor_ref[...] = columns(factors / total)
    own = factor_ref[pl.ds(pl.multiple_of(at_ref[0] * CHUNK, CHUNK), CHUNK), :]
    out = jnp.zeros((CHUNK, HEAD_DIM), jnp.float32)
    for i in range(count):
        out += own[:, i : i + 1] * parts[i, :CHUNK, :]
    out_ref[...] = out.astype(jnp.bfloat16)


def merge(at, parts):
    return pl.pallas_call(
        merge_kernel,
        out_shape=jax.ShapeDtypeStruct((CHUNK, HEAD_DIM), jnp.bfloat16),
        in_specs=[smem(), vmem()],
        out_specs=vmem(),
        scratch_shapes=[pltpu.VMEM((STACKED, HEAD_DIM), jnp.float32)],
        compiler_params=params(),
    )(at, parts)


def place_kernel(core_ref, near_ref, far_ref, out_ref):
    per_head = QUERIES // CHUNK
    for at in range(HEADS):
        head = jnp.bitwise_xor(core_ref[0] * (HEADS // NC), at)
        lanes = pl.ds(pl.multiple_of(head * HEAD_DIM, HEAD_DIM), HEAD_DIM)
        source = near_ref if at < HEADS // NC else far_ref
        lo = at % (HEADS // NC) * per_head
        for i in range(per_head):
            out_ref[i * CHUNK : (i + 1) * CHUNK, lanes] = source[lo + i]


def place(core, near, far):
    return pl.pallas_call(
        place_kernel,
        out_shape=jax.ShapeDtypeStruct((QUERIES, HEADS * HEAD_DIM), jnp.bfloat16),
        in_specs=[smem(), vmem(), vmem()],
        out_specs=vmem(),
        compiler_params=params(),
    )(core, near, far)


def summed(keep, send):
    part = (keep + across(send)).reshape(NY * NZ, -1, 4, HEAD_DIM)
    near = gather(jnp.sum(scatter(part), axis=0)).reshape(HALF * RANK, HEAD_DIM)
    return near, across(near)


def shards(cache_keys, cache_values, sketch_matrix, queries, visible):
    shard_rows = cache_keys.shape[0]
    me = lax.axis_index("ctx").astype(jnp.int32)
    core = (me % NC).reshape(1)
    near, far = summed(*local_power(core, cache_keys, pltpu.with_memory_space_constraint(sketch_matrix.T, pltpu.HBM)))
    limit = visible.reshape(QUERIES, 1) - me * shard_rows
    rank_keys, keep, send = attend(
        core, near, far, cache_keys, cache_values, queries.reshape(QUERIES, -1), limit
    )
    parts = scatter(merge_pair(keep, across(send)))
    chunk = merge((me // NC % (STACKED // CHUNK)).reshape(1), parts)
    near = gather(chunk)
    attended = place(core, near, across(near))
    return rank_keys.T, attended.reshape(STEPS, ROWS, HEADS * HEAD_DIM)


def solution(mesh):
    in_specs = (P("ctx", "batch"), P("ctx", "batch"), P(), P(None, "batch", None), P(None, "batch"))
    out_specs = (P("ctx", "batch"), P(None, "batch", None))
    return jax.shard_map(shards, mesh=mesh, in_specs=in_specs, out_specs=out_specs, check_vma=False)
```

```python
import math

import jax
import jax.numpy as jnp
from jax import lax
from jax.experimental import pallas as pl
from jax.experimental.pallas import tpu as pltpu
from jax.sharding import PartitionSpec as P

HEADS = 32
KV_HEADS = 8
HEAD_DIM = 128
RANK = 160
ROWS = 16
STEPS = 2
WIDTH = KV_HEADS * HEAD_DIM
GROUP = HEADS // KV_HEADS
QUERIES = STEPS * ROWS
STACKED = GROUP * QUERIES
NY = 4
NZ = 8
NC = 2
HALF = KV_HEADS // NC
CHUNK = HALF * STACKED // (NY * NZ)
SPLIT = 3
EXTRA = 8
VMEM_BYTES = 50 * 1024 * 1024
HIGH = lax.Precision.HIGHEST
BLOCK = 32
PANEL = 8
LANES = 128
SPARE = RANK - LANES
LOG_SCALE = math.log2(math.e) / math.sqrt(HEAD_DIM)
HIDDEN = -1e30


def params():
    return pltpu.CompilerParams(vmem_limit_bytes=VMEM_BYTES)


def vmem():
    return pl.BlockSpec(memory_space=pltpu.VMEM)


def hbm():
    return pl.BlockSpec(memory_space=pltpu.HBM)


def smem():
    return pl.BlockSpec(memory_space=pltpu.SMEM)


def nn(a, b, precision=None):
    return jnp.dot(a, b, precision=precision, preferred_element_type=jnp.float32)


def nt(a, b, precision=None):
    return lax.dot_general(
        a, b, (((1,), (1,)), ((), ())), precision=precision, preferred_element_type=jnp.float32
    )


def tn(a, b, precision=None):
    return lax.dot_general(
        a, b, (((0,), (0,)), ((), ())), precision=precision, preferred_element_type=jnp.float32
    )


def index(y, z, c):
    return (y * NZ + z) * NC + c


CORES = [[index(y, z, c) for y in range(NY) for z in range(NZ)] for c in range(NC)]


def across(x):
    pairs = [(i, i ^ 1) for i in range(NY * NZ * NC)]
    return lax.ppermute(x, "ctx", pairs)


def scatter(x):
    return lax.all_to_all(x, "ctx", 0, 0, axis_index_groups=CORES)


def gather(x):
    return scatter(jnp.broadcast_to(x, (NY * NZ, *x.shape)))


def power_kernel(
    core_ref, keys_ref, sketch_hbm, keep_ref, send_ref, keys_buf, sketch_ref, total_ref, sems, *, pieces
):
    block = keys_buf.shape[0] // pieces
    copies = []
    for i in range(pieces):
        rows = pl.ds(i * block, block)
        copies.append(
            pltpu.make_async_copy(keys_ref.at[rows, :], keys_buf.at[rows, :], sems.at[i])
        )
    copies.append(pltpu.make_async_copy(sketch_hbm, sketch_ref, sems.at[pieces]))
    for copy in (copies[pieces], *copies[:pieces]):
        copy.start()
    copies[pieces].wait()
    total, rows = None, None
    for i in range(pieces + 1):
        before = rows
        if i < pieces:
            copies[i].wait()
            keys = keys_buf[i * block : (i + 1) * block, :]
            rows = nt(keys, sketch_ref[...]).astype(jnp.bfloat16)
        if i:
            part = tn(before, keys_buf[(i - 1) * block : i * block, :])
            total = part if total is None else total + part
    total_ref[...] = total
    for at in range(KV_HEADS):
        group = jnp.bitwise_xor(core_ref[0] * HALF, at)
        lane = pl.multiple_of(group * HEAD_DIM, HEAD_DIM)
        out_ref = keep_ref if at < HALF else send_ref
        lo = at % HALF * RANK
        out_ref[lo : lo + RANK, :] = total_ref[:, pl.ds(lane, HEAD_DIM)]


def local_power(core, keys, sketch):
    positions = keys.shape[0]
    pieces = 4
    half = jax.ShapeDtypeStruct((HALF * RANK, HEAD_DIM), jnp.float32)
    return pl.pallas_call(
        lambda *refs: power_kernel(*refs, pieces=pieces),
        in_specs=[smem(), hbm(), hbm()],
        out_specs=[vmem(), vmem()],
        out_shape=[half, half],
        scratch_shapes=[
            pltpu.VMEM((positions, WIDTH), jnp.bfloat16),
            pltpu.VMEM((RANK, WIDTH), jnp.bfloat16),
            pltpu.VMEM((RANK, WIDTH), jnp.float32),
            pltpu.SemaphoreType.DMA((pieces + 1,)),
        ],
        compiler_params=params(),
    )(core, keys, sketch)


def deep(left, right, axis):
    (a, b, c), (d, e, f) = split(left, 3), split(right, 3)
    return jnp.concatenate([a, a, b, b, a, c], axis), jnp.concatenate([d, e, d, e, f, d], 0)


def eliminate(tiles, start):
    below = lax.broadcasted_iota(jnp.int32, (BLOCK, LANES), 0)
    done = []
    for panel in range(0, BLOCK, PANEL):
        at = start + panel
        own = tiles[at // LANES]
        columns = [
            jnp.broadcast_to(own[:, (at + j) % LANES : (at + j) % LANES + 1], own.shape)
            for j in range(PANEL)
        ]
        for j in range(PANEL):
            ratio = columns[j] * (1.0 / columns[j][j : j + 1])
            ratio = jnp.where(below[: BLOCK - panel] > j, ratio, 0.0)
            for m in range(j + 1, PANEL):
                columns[m] = columns[m] - ratio * columns[m][j : j + 1]
            tiles = [tile - ratio * tile[j : j + 1] for tile in tiles]
        done.append([tile[:PANEL] for tile in tiles])
        tiles = [tile[PANEL:] for tile in tiles]
    return [jnp.concatenate(pieces, axis=0) for pieces in zip(*done)]


def factor_inverse(gram, work_ref):
    row = lax.broadcasted_iota(jnp.int32, (BLOCK, LANES), 0)
    lane = lax.broadcasted_iota(jnp.int32, (BLOCK, LANES), 1)
    wide = lax.broadcasted_iota(jnp.int32, (RANK, 2 * LANES), 1)
    work_ref[...] = jnp.zeros_like(work_ref)
    work_ref[:, :RANK] = gram
    for lo in range(0, RANK, BLOCK):
        hi = lo + BLOCK
        own, offset = lo // LANES, lo % LANES
        identity = jnp.where(lane == row + SPARE, 1.0, 0.0)
        tiles = [work_ref[lo:hi, :LANES], work_ref[lo:hi, LANES:] + identity]
        tiles = eliminate(tiles, lo)
        moved = pltpu.roll(tiles[1], (offset - SPARE) % LANES, 1)
        tiles[1] = jnp.where(lane < SPARE, tiles[1], 0.0)
        diagonal = jnp.sum(jnp.where(lane == row + offset, tiles[own], 0.0), axis=1, keepdims=True)
        root = lax.rsqrt(diagonal)
        root = root * (1.5 - 0.5 * (diagonal * root) * root)
        inside = (lane >= offset) & (lane < offset + BLOCK)
        tiles[own] = jnp.where(inside, moved, tiles[own])
        rows = jnp.concatenate(tiles, axis=1) * root
        work_ref[lo:hi, :] = rows
        if hi < RANK:
            left = wide[hi:]
            rest = jnp.where((left >= lo) & (left < hi), 0.0, work_ref[hi:, :])
            work_ref[hi:, :] = rest - tn(*deep(rows[:, hi:RANK], rows, 0))
    row = lax.broadcasted_iota(jnp.int32, (RANK, 2 * LANES), 0)
    return jnp.where(wide <= row, work_ref[...], 0.0)[:, :RANK]


def split(x, count):
    out = []
    for _ in range(count):
        out.append(x.astype(jnp.bfloat16))
        x = x - out[-1].astype(jnp.float32)
    return out


def find_basis(core_ref, near_ref, far_ref, basis_ref, power_ref, work_ref):
    for at in range(KV_HEADS):
        group = jnp.bitwise_xor(core_ref[0] * HALF, at)
        lanes = pl.ds(pl.multiple_of(group * HEAD_DIM, HEAD_DIM), HEAD_DIM)
        source = near_ref if at < HALF else far_ref
        lo = at % HALF * RANK
        power_ref[:, lanes] = source[lo : lo + RANK, :]
    high, middle, low = split(power_ref[...], 3)
    cross = nt(high, middle) + nt(high, low)
    gram = nt(high, high) + (nt(middle, middle) + (cross + cross.T))
    inverse = factor_inverse(gram, work_ref)
    first, second = split(inverse, 2), (high, middle)
    left = jnp.concatenate([first[0], first[0], first[1]], axis=1)
    right = jnp.concatenate([second[0], second[1], second[0]], axis=0)
    basis_ref[...] = nn(left, right).astype(jnp.bfloat16)


def attend_kernel(
    core_ref,
    near_ref,
    far_ref,
    keys_ref,
    values_ref,
    queries_ref,
    limit_ref,
    rank_ref,
    keep_ref,
    send_ref,
    basis_ref,
    power_ref,
    work_ref,
    keys_buf,
    values_buf,
    masked_ref,
    projected_ref,
    scores_ref,
    sems,
):
    copies = [
        pltpu.make_async_copy(keys_ref, keys_buf, sems.at[0]),
        pltpu.make_async_copy(masked_ref.at[pl.ds(0, RANK), :], rank_ref, sems.at[1]),
    ]
    for half in range(NC):
        first = jnp.bitwise_xor(core_ref[0], 1 - half) * HALF * HEAD_DIM
        lanes = pl.ds(pl.multiple_of(first, HALF * HEAD_DIM), HALF * HEAD_DIM)
        copies.append(
            pltpu.make_async_copy(
                values_ref.at[:, lanes], values_buf.at[:, lanes], sems.at[2 + half]
            )
        )
    for copy in (copies[0], copies[2], copies[3]):
        copy.start()
    positions = keys_buf.shape[0]
    column = lax.broadcasted_iota(jnp.int32, (QUERIES, positions), 1)
    masked_ref[RANK:, :] = jnp.where(column < limit_ref[...], 0.0, HIDDEN).astype(jnp.bfloat16)
    row = lax.broadcasted_iota(jnp.int32, (STACKED, QUERIES), 0)
    lane = lax.broadcasted_iota(jnp.int32, (STACKED, QUERIES), 1)
    own_mask = jnp.where(row % QUERIES == lane, 1.0, 0.0).astype(jnp.bfloat16)
    find_basis(core_ref, near_ref, far_ref, basis_ref, power_ref, work_ref)
    copies[0].wait()
    for lo in range(0, positions, positions // 4):
        hi = lo + positions // 4
        rank = nt(basis_ref[...], keys_buf[lo:hi, :])
        masked_ref[:RANK, lo:hi] = rank.astype(jnp.bfloat16)
    copies[1].start()
    lane = lax.broadcasted_iota(jnp.int32, (STACKED, HEAD_DIM), 1)
    for half, out_ref in enumerate((send_ref, keep_ref)):
        start = jnp.bitwise_xor(core_ref[0], 1 - half) * HALF
        for at in range(HALF):
            g = start + at
            stacked = []
            for q in range(GROUP):
                own = pl.ds(pl.multiple_of((g * GROUP + q) * HEAD_DIM, HEAD_DIM), HEAD_DIM)
                stacked.append(queries_ref[:, own])
            stacked = jnp.concatenate(stacked, axis=0)
            lanes = pl.ds(pl.multiple_of(g * HEAD_DIM, HEAD_DIM), HEAD_DIM)
            rows = slice(at * STACKED, (at + 1) * STACKED)
            projected = nt(stacked, basis_ref[:, lanes]).astype(jnp.bfloat16)
            projected_ref[half, rows, :RANK] = projected
            projected_ref[half, rows, RANK:] = own_mask
        for lo in range(0, positions, positions // 4):
            hi = lo + positions // 4
            scores_ref[half, :, lo:hi] = nn(projected_ref[half], masked_ref[:, lo:hi])
        copies[2 + half].wait()
        extras = jnp.zeros((STACKED, HEAD_DIM), jnp.float32)
        for pair in range(0, HALF, 2):
            weights = []
            for at in (pair, pair + 1):
                scores = scores_ref[half, at * STACKED : (at + 1) * STACKED, :]
                top = jnp.max(scores, axis=1, keepdims=True)
                expo = jnp.exp2((scores - top) * LOG_SCALE)
                total = jnp.sum(expo, axis=1, keepdims=True)
                weights.append(expo.astype(jnp.bfloat16))
                extras = jnp.where(lane == 2 * at, top * LOG_SCALE, extras)
                extras = jnp.where(lane == 2 * at + 1, total, extras)
            lanes = pl.ds(pl.multiple_of((start + pair) * HEAD_DIM, 2 * HEAD_DIM), 2 * HEAD_DIM)
            both = nn(jnp.concatenate(weights, axis=0), values_buf[:, lanes])
            out_ref[pair, :STACKED, :] = both[:STACKED, :HEAD_DIM]
            out_ref[pair + 1, :STACKED, :] = both[STACKED:, HEAD_DIM:]
        extras = extras.T
        for at in range(HALF):
            row = extras[2 * at : 2 * at + 2]
            out_ref[at, STACKED:, :] = jnp.concatenate([row] * (EXTRA // 2), axis=0)
    copies[1].wait()


def attend(core, near, far, keys, values, queries, limit):
    positions = keys.shape[0]
    return pl.pallas_call(
        attend_kernel,
        out_shape=[
            jax.ShapeDtypeStruct((RANK, positions), jnp.bfloat16),
            *[jax.ShapeDtypeStruct((HALF, STACKED + EXTRA, HEAD_DIM), jnp.float32)] * 2,
        ],
        in_specs=[smem(), vmem(), vmem(), hbm(), hbm(), vmem(), vmem()],
        out_specs=[hbm(), vmem(), vmem()],
        scratch_shapes=[
            pltpu.VMEM((RANK, WIDTH), jnp.bfloat16),
            pltpu.VMEM((RANK, WIDTH), jnp.float32),
            pltpu.VMEM((RANK, 2 * LANES), jnp.float32),
            pltpu.VMEM((positions, WIDTH), jnp.bfloat16),
            pltpu.VMEM((positions, WIDTH), jnp.bfloat16),
            pltpu.VMEM((RANK + QUERIES, positions), jnp.bfloat16),
            pltpu.VMEM((NC, HALF * STACKED, RANK + QUERIES), jnp.bfloat16),
            pltpu.VMEM((NC, HALF * STACKED, positions), jnp.float32),
            pltpu.SemaphoreType.DMA((4,)),
        ],
        compiler_params=params(),
    )(core, near, far, keys, values, queries, limit)


def columns(rows):
    pad = jnp.zeros((HEAD_DIM - rows.shape[0], rows.shape[1]), jnp.float32)
    return jnp.concatenate([rows, pad], axis=0).T


def terms(x):
    return [term.astype(jnp.float32) for term in split(x, SPLIT)]


def pair_kernel(keep_ref, sent_ref, out_ref):
    chunks = STACKED // CHUNK
    rest = jnp.zeros((EXTRA - 2 * SPLIT, STACKED), jnp.float32)
    factors, extras = [], []
    for g in range(HALF):
        tops = [ref[g, STACKED : STACKED + 1, :] for ref in (keep_ref, sent_ref)]
        totals = [ref[g, STACKED + 1 : STACKED + 2, :] for ref in (keep_ref, sent_ref)]
        top = jnp.maximum(*tops)
        pair = [jnp.exp2(t - top) for t in tops]
        total = pair[0] * totals[0] + pair[1] * totals[1]
        extras.append(jnp.concatenate([*terms(top), *terms(total), rest], axis=0))
        factors += pair
    factors = columns(jnp.concatenate(factors, axis=0))
    for g in range(HALF):
        numerator = factors[:, 2 * g : 2 * g + 1] * keep_ref[g, :STACKED]
        numerator += factors[:, 2 * g + 1 : 2 * g + 2] * sent_ref[g, :STACKED]
        for i in range(chunks):
            rows = numerator[i * CHUNK : (i + 1) * CHUNK]
            part = jnp.concatenate([rows, extras[g]], axis=0)
            out_ref[g * chunks + i] = part.astype(jnp.bfloat16)


def merge_pair(keep, sent):
    return pl.pallas_call(
        pair_kernel,
        out_shape=jax.ShapeDtypeStruct((NY * NZ, CHUNK + EXTRA, HEAD_DIM), jnp.bfloat16),
        in_specs=[vmem(), vmem()],
        out_specs=vmem(),
        compiler_params=params(),
    )(keep, sent)


def merge_kernel(at_ref, parts_ref, out_ref, factor_ref):
    count = parts_ref.shape[0]
    parts = parts_ref[...].astype(jnp.float32)
    extra = parts[:, CHUNK:, :]
    tops = sum(extra[:, i, :] for i in range(SPLIT))
    totals = sum(extra[:, SPLIT + i, :] for i in range(SPLIT))
    factors = jnp.exp2(tops - jnp.max(tops, axis=0, keepdims=True))
    total = jnp.sum(factors * totals, axis=0, keepdims=True)
    factor_ref[...] = columns(factors / total)
    own = factor_ref[pl.ds(pl.multiple_of(at_ref[0] * CHUNK, CHUNK), CHUNK), :]
    out = jnp.zeros((CHUNK, HEAD_DIM), jnp.float32)
    for i in range(count):
        out += own[:, i : i + 1] * parts[i, :CHUNK, :]
    out_ref[...] = out.astype(jnp.bfloat16)


def merge(at, parts):
    return pl.pallas_call(
        merge_kernel,
        out_shape=jax.ShapeDtypeStruct((CHUNK, HEAD_DIM), jnp.bfloat16),
        in_specs=[smem(), vmem()],
        out_specs=vmem(),
        scratch_shapes=[pltpu.VMEM((STACKED, HEAD_DIM), jnp.float32)],
        compiler_params=params(),
    )(at, parts)


def place_kernel(core_ref, near_ref, far_ref, out_ref):
    per_head = QUERIES // CHUNK
    for at in range(HEADS):
        head = jnp.bitwise_xor(core_ref[0] * (HEADS // NC), at)
        lanes = pl.ds(pl.multiple_of(head * HEAD_DIM, HEAD_DIM), HEAD_DIM)
        source = near_ref if at < HEADS // NC else far_ref
        lo = at % (HEADS // NC) * per_head
        for i in range(per_head):
            out_ref[i * CHUNK : (i + 1) * CHUNK, lanes] = source[lo + i]


def place(core, near, far):
    return pl.pallas_call(
        place_kernel,
        out_shape=jax.ShapeDtypeStruct((QUERIES, HEADS * HEAD_DIM), jnp.bfloat16),
        in_specs=[smem(), vmem(), vmem()],
        out_specs=vmem(),
        compiler_params=params(),
    )(core, near, far)


def summed(keep, send):
    part = (keep + across(send)).reshape(NY * NZ, -1, 4, HEAD_DIM)
    near = gather(jnp.sum(scatter(part), axis=0)).reshape(HALF * RANK, HEAD_DIM)
    return near, across(near)


def shards(cache_keys, cache_values, sketch_matrix, queries, visible):
    shard_rows = cache_keys.shape[0]
    me = lax.axis_index("ctx").astype(jnp.int32)
    core = (me % NC).reshape(1)
    near, far = summed(*local_power(core, cache_keys, pltpu.with_memory_space_constraint(sketch_matrix.T, pltpu.HBM)))
    limit = visible.reshape(QUERIES, 1) - me * shard_rows
    rank_keys, keep, send = attend(
        core, near, far, cache_keys, cache_values, queries.reshape(QUERIES, -1), limit
    )
    parts = scatter(merge_pair(keep, across(send)))
    chunk = merge((me // NC % (STACKED // CHUNK)).reshape(1), parts)
    near = gather(chunk)
    attended = place(core, near, across(near))
    return rank_keys.T, attended.reshape(STEPS, ROWS, HEADS * HEAD_DIM)


def solution(mesh):
    in_specs = (P("ctx", "batch"), P("ctx", "batch"), P(), P(None, "batch", None), P(None, "batch"))
    out_specs = (P("ctx", "batch"), P(None, "batch", None))
    return jax.shard_map(shards, mesh=mesh, in_specs=in_specs, out_specs=out_specs, check_vma=False)
```
